128 devices in a mesh: region: 4 (over z), brick: 32 (over x, y, core).
Axes of the slice: x: 4, y: 4, z: 4, core: 2. Of those that a mesh axis runs over, the one named last changes fastest.
Arguments:
- features: bfloat16 [512, 64, 512], P(('region', 'brick')), may hold values from -6 to 6
- active: int32 [512, 512], P(('region', 'brick')), may hold values 0 or 1
- neighbours: int32 [512, 26], P(('region', 'brick')), may hold values from -1 to 511, as said below
- first_weight: bfloat16 [27, 64, 64], replicated, may hold values from -0.15625 to 0.15625
- second_weight: bfloat16 [27, 64, 64], replicated, may hold values from -0.15625 to 0.15625
- film_scale: float32 [64], replicated, may hold values from -0.5 to 0.5
- film_shift: float32 [64], replicated, may hold values from -3 to 3
- cotangent: bfloat16 [512, 64, 512], P(('region', 'brick')), may hold values from -0.109375 to 0.109375
Outputs:
- block_output: bfloat16 [512, 64, 512], P(('region', 'brick'))
- grad_first: float32 [27, 64, 64], replicated
- grad_second: float32 [27, 64, 64], replicated
The draws below stay inside these ranges and needn't reach their ends.
Inputs may be any that keep to these rules, and one draw needn't show every extreme that they name: neighbours[b, e] is the brick adjoining brick b at offset e (numbered as in the reference program) or -1. The lists are symmetric: neighbours[b, e] = n >= 0 exactly when neighbours[n, e'] = b for the opposite offset e' = -e. Brick b is stored on the device of index b // 4 over region+brick. The devices of one region index form a grid of 8 columns by 4 rows, brick index = row * 8 + column, and every listed neighbour lies on the same device or on one of the eight devices whose column and row differ by at most one. The face of n read at offset e is n's face on the side of the first nonzero component of -e; counting distinct pairs (brick n, that face) that bricks of one device read from bricks of another, no pair of devices beside each other along columns has more than 4, along rows more than 2, diagonally more than 2, and in every draw some pair of each of these three kinds has exactly that many.
All inputs are finite; a program needn't handle non-finite values. No bound on the sum of `active` on one device may be relied on, other than what follows from the above.
Results may differ from the reference program's by a relative error of at most 0.0054.
Values may be sent and summed in bfloat16 or wider, within the bound.
No kernel may reach another device: no remote copies, remote signals or barrier semaphores. Data moves between devices by JAX's collectives and lax.ppermute only.
A program may use at most 128 MiB of HBM per device.

```python
import jax
import jax.numpy as jnp
import numpy as np
from jax import lax

C = 64
BX = 1
BY = 2
BZ = 2
B_DEV = 4
NBRICKS = 512
N_REGION = 4
N_BRICK = 32
DEVICES = 128


def draw_neighbours(key, part):
    key = jax.random.fold_in(key, 11)
    columns = N_BRICK // 4
    span_x = columns * BX
    span_y = 4 * BY
    span_z = BZ
    link_key, pick_key = jax.random.split(key)
    link_bits = jax.random.randint(link_key, (N_REGION, span_x + 2, span_y + 2, span_z + 2, 27), 0, 4) > 0
    picks = jax.random.randint(pick_key, (6,), 0, 1 << 20)
    region_x = picks[0] % N_REGION
    column_x = picks[1] % (columns - 1)
    row_x = picks[2] % 4
    region_y = picks[3] % N_REGION
    column_y = picks[4] % columns
    row_y = picks[5] % 3
    bricks_dev = BX * BY * BZ
    global_id = jnp.arange(N_REGION * N_BRICK * bricks_dev)
    region = global_id // (N_BRICK * bricks_dev)
    device = global_id // bricks_dev % N_BRICK
    local_index = global_id % bricks_dev
    my_column = device % columns
    my_row = device // columns
    pos_x = my_column * BX + local_index // (BY * BZ)
    pos_y = my_row * BY + local_index // BZ % BY
    pos_z = local_index % BZ
    results = []
    for a in (-1, 0, 1):
        for b in (-1, 0, 1):
            for c in (-1, 0, 1):
                if (a, b, c) == (0, 0, 0):
                    continue
                near_x = pos_x + a
                near_y = pos_y + b
                near_z = pos_z + c
                inside = (near_x >= 0) & (near_x < span_x) & (near_y >= 0) & (near_y < span_y) & (near_z >= 0) & (near_z < span_z)
                leading = a if a != 0 else b if b != 0 else c
                if leading > 0:
                    link_bit = link_bits[region, pos_x + 1, pos_y + 1, pos_z + 1, (a + 1) * 9 + (b + 1) * 3 + (c + 1)]
                else:
                    link_bit = link_bits[region, near_x + 1, near_y + 1, near_z + 1, (1 - a) * 9 + (1 - b) * 3 + (1 - c)]
                clip_x = jnp.clip(near_x, 0, span_x - 1)
                clip_y = jnp.clip(near_y, 0, span_y - 1)
                clip_z = jnp.clip(near_z, 0, span_z - 1)
                near_column = clip_x // BX
                near_row = clip_y // BY
                forced_x = (region == region_x) & (my_row == row_x) & (near_row == row_x) & ((my_column == column_x) & (near_column == column_x + 1) | (my_column == column_x + 1) & (near_column == column_x))
                forced_y = (region == region_y) & (my_column == column_y) & (near_column == column_y) & ((my_row == row_y) & (near_row == row_y + 1) | (my_row == row_y + 1) & (near_row == row_y))
                forced_d = (region == region_y) & ((my_column == column_x) & (my_row == row_y) & (near_column == column_x + 1) & (near_row == row_y + 1) | (my_column == column_x + 1) & (my_row == row_y + 1) & (near_column == column_x) & (near_row == row_y))
                linked = inside & (link_bit | forced_x | forced_y | forced_d)
                near_device = near_row * columns + near_column
                near_local = (clip_x % BX * BY + clip_y % BY) * BZ + clip_z
                near_id = (region * N_BRICK + near_device) * bricks_dev + near_local
                results.append(jnp.where(linked, near_id, -1))
    return jnp.stack(results, axis=1).astype(jnp.int32)


def touch_ends(drawn, own_key, smallest, top_value):
    longest = drawn.shape.index(max(drawn.shape))
    spots = []
    for shift in (0, 1):
        where = [jax.random.randint(jax.random.fold_in(own_key, axis), (), 0, length) for axis, length in enumerate(drawn.shape)]
        where[longest] = (where[longest] + shift) % drawn.shape[longest]
        spots.append(tuple(where))
    return drawn.at[spots[0]].set(smallest).at[spots[1]].set(top_value)


def shard_levels(rng, dims, cuts, least, top_value):
    level, own = 1.0, jax.random.fold_in(rng, 6)
    for dim, parts in cuts:
        heights = jnp.exp(jax.random.uniform(jax.random.fold_in(own, dim), (parts,), jnp.float32, least / len(cuts), top_value / len(cuts)))
        level = level * jnp.repeat(heights, dims[dim] // parts).reshape([-1 if axis == dim else 1 for axis in range(len(dims))])
    return level


def normal_values(stream_key, dims, spread, limit, cuts=(), kind=jnp.bfloat16):
    drawn = spread * jax.random.normal(stream_key, dims, jnp.float32)
    if cuts:
        drawn = drawn * shard_levels(stream_key, dims, cuts, -0.22, 0.18)
    return jnp.clip(drawn, -limit, limit).astype(kind)


def setup_inputs(seed: int = 0) -> dict:
    splits = jax.random.split(jax.random.key(seed), 9)
    return {
        "features": normal_values(splits[0], (NBRICKS, C, 512), 1.0, 6.0, ((0, 128),)),
        "active": touch_ends((jax.random.randint(splits[1], (NBRICKS, 512), 0, 8) < 5).astype(jnp.int32), jax.random.fold_in(splits[1], 1), 0, 1),
        "neighbours": draw_neighbours(jax.random.fold_in(splits[8], 71), 0),
        "first_weight": normal_values(splits[3], (27, C, C), (27 * C) ** -0.5, 0.15625),
        "second_weight": normal_values(splits[4], (27, C, C), (27 * C) ** -0.5, 0.15625),
        "film_scale": jnp.clip(jax.random.uniform(splits[5], (C,), jnp.float32, -0.5, 0.5), -0.5, 0.5),
        "film_shift": normal_values(splits[6], (C,), 0.5, 3.0, (), jnp.float32),
        "cotangent": normal_values(splits[7], (NBRICKS, C, 512), (3.0 / (B_DEV * DEVICES * 320) ** 0.5), 0.109375, ((0, 128),)),
    }


def direction_list():
    return [(a, b, c) for a in (-1, 0, 1) for b in (-1, 0, 1) for c in (-1, 0, 1) if (a, b, c) != (0, 0, 0)]

def face_of(vector):
    if vector[0] != 0:
        return 0 if vector[0] < 0 else 1
    if vector[1] != 0:
        return 2 if vector[1] < 0 else 3
    return 4 if vector[2] < 0 else 5

def face_voxels():
    lookup = np.zeros((6, 64), np.int32)
    for face_index in range(6):
        axis_index = face_index // 2
        others = [i for i in range(3) if i != axis_index]
        for outer_cell in range(8):
            for inner_cell in range(8):
                coords = [0, 0, 0]
                coords[axis_index] = 7 if face_index % 2 else 0
                coords[others[0]] = outer_cell
                coords[others[1]] = inner_cell
                lookup[face_index, outer_cell * 8 + inner_cell] = coords[0] * 64 + coords[1] * 8 + coords[2]
    return lookup.reshape(-1)

def halo_tables():
    directions = direction_list()
    cell_lists = [[] for _ in directions]
    place_lists = [[] for _ in directions]
    source = np.zeros(1000, np.int32)
    for position in range(1000):
        padded = (position // 100, position // 10 % 10, position % 10)
        vector = tuple((-1 if t == 0 else 1 if t == 9 else 0 for t in padded))
        if vector == (0, 0, 0):
            source[position] = (padded[0] - 1) * 64 + (padded[1] - 1) * 8 + padded[2] - 1
            continue
        direction_index = directions.index(vector)
        coords = [7 if vector[i] < 0 else 0 if vector[i] > 0 else padded[i] - 1 for i in range(3)]
        face_index = face_of(tuple((-t for t in vector)))
        others = [i for i in range(3) if i != face_index // 2]
        cell_lists[direction_index].append(coords[others[0]] * 8 + coords[others[1]])
        place_lists[direction_index].append(position)
    offset = 512
    for direction_index in range(len(directions)):
        for position in place_lists[direction_index]:
            source[position] = offset
            offset += 1
    read_faces = np.array([face_of(tuple((-t for t in d))) for d in directions], np.int32)
    return ([np.array(c, np.int32) for c in cell_lists], source, read_faces)

def face_pool(values):
    total_bricks, channels = (values.shape[0], values.shape[1])
    faces = jnp.take(values, jnp.asarray(face_voxels()), axis=2)
    faces = faces.reshape(total_bricks, channels, 6, 64).transpose(0, 2, 1, 3).reshape(total_bricks * 6, channels, 64)
    return jnp.concatenate([faces, jnp.zeros((1, channels, 64), values.dtype)], axis=0)

def padded_block(face_table, own_values, link_rows, cell_lists, source, read_faces):
    zero_row = face_table.shape[0] - 1
    pieces = [own_values]
    for direction_index in range(26):
        links = link_rows[:, direction_index].astype(jnp.int32)
        row_index = jnp.where(links >= 0, links * 6 + int(read_faces[direction_index]), zero_row).astype(jnp.int32)
        face_rows = jnp.take(face_table, row_index, axis=0)
        pieces.append(jnp.take(face_rows, jnp.asarray(cell_lists[direction_index]), axis=2))
    joined = jnp.concatenate(pieces, axis=2)
    return jnp.take(joined, jnp.asarray(source), axis=2)

def kernel_of(weight):
    channels = weight.shape[1]
    return weight.reshape(3, 3, 3, channels, channels).transpose(3, 4, 0, 1, 2)

def flipped_of(weight):
    channels = weight.shape[1]
    return weight.reshape(3, 3, 3, channels, channels)[::-1, ::-1, ::-1].transpose(4, 3, 0, 1, 2)

def correlate(padded, kernel):
    return lax.conv_general_dilated(padded, kernel, (1, 1, 1), 'VALID', dimension_numbers=('NCDHW', 'OIDHW', 'NCDHW'), precision=lax.Precision.HIGHEST)

def reference(features, active, neighbours, first_weight, second_weight, film_scale, film_shift, cotangent):
    total_bricks, channels = (features.shape[0], features.shape[1])
    blocks = total_bricks // B_DEV
    cell_lists, source, read_faces = halo_tables()
    active_mask = active.astype(jnp.float32)[:, None, :]

    def blocked(array):
        return array.reshape((blocks, B_DEV) + array.shape[1:])

    def padded_of(values):
        face_table = face_pool(values)

        def single(own_values, link_rows):
            flat_padded = padded_block(face_table, own_values, link_rows, cell_lists, source, read_faces)
            return flat_padded.astype(jnp.float32).reshape(own_values.shape[0], channels, 10, 10, 10)
        return single

    def convolve(values, kernel):
        padder = padded_of(values)

        def single(operands):
            result = correlate(padder(operands[0], operands[1]), kernel)
            return result.reshape(B_DEV, channels, 512)
        return lax.map(single, (blocked(values), blocked(neighbours))).reshape(total_bricks, channels, 512)

    def weight_grad(values, slope, weight):
        padder = padded_of(values)

        def single(triple):
            padded = padder(triple[0], triple[1])
            target = triple[2].astype(jnp.float32).reshape(B_DEV, channels, 8, 8, 8)
            pullback = jax.vjp(lambda w: correlate(padded, kernel_of(w)), weight)[1]
            return pullback(target)[0]
        return lax.optimization_barrier(jnp.sum(lax.map(single, (blocked(values), blocked(neighbours), blocked(slope))), axis=0))
    activated = (active_mask * jax.nn.silu(features.astype(jnp.float32))).astype(jnp.bfloat16)
    first_float = first_weight.astype(jnp.float32)
    second_float = second_weight.astype(jnp.float32)
    pre_first = convolve(activated, kernel_of(first_float))
    film_gain = 1.0 + film_scale[None, :, None]
    shaped = pre_first * film_gain + film_shift[None, :, None]
    hidden = (active_mask * jax.nn.silu(shaped)).astype(jnp.bfloat16)
    second = convolve(hidden, kernel_of(second_float))
    block_output = (features.astype(jnp.float32) + active_mask * second).astype(jnp.bfloat16)
    slope_second = (active_mask * cotangent.astype(jnp.float32)).astype(jnp.bfloat16)
    grad_second = weight_grad(hidden, slope_second, second_float)
    back_hidden = convolve(slope_second, flipped_of(second_float))
    sigmoid_gate = jax.nn.sigmoid(shaped)
    slope_first = (back_hidden * active_mask * sigmoid_gate * (1.0 + shaped * (1.0 - sigmoid_gate)) * film_gain).astype(jnp.bfloat16)
    grad_first = weight_grad(activated, slope_first, first_float)
    return (block_output, grad_first, grad_second)
```

```python
import jax
import jax.numpy as jnp
import numpy as np
from jax import lax
from jax.experimental import pallas as pl
from jax.experimental.pallas import tpu as pltpu
from jax.sharding import PartitionSpec as P

AXES = ("region", "brick")
GRID_X = 8
ZERO_ROW = 44
ARRIVALS = {
    (-1, 0): (24, 4),
    (1, 0): (28, 4),
    (0, -1): (32, 2),
    (-1, -1): (34, 2),
    (1, -1): (36, 2),
    (0, 1): (38, 2),
    (-1, 1): (40, 2),
    (1, 1): (42, 2),
}
VMEM_LIMIT = 48 * 1024 * 1024
BF = jnp.bfloat16
F32 = jnp.float32


def direction_list():
    return [
        (a, b, c)
        for a in (-1, 0, 1)
        for b in (-1, 0, 1)
        for c in (-1, 0, 1)
        if (a, b, c) != (0, 0, 0)
    ]


DIRECTIONS = direction_list()


def face_of(vector):
    if vector[0] != 0:
        return 0 if vector[0] < 0 else 1
    if vector[1] != 0:
        return 2 if vector[1] < 0 else 3
    return 4 if vector[2] < 0 else 5


SEND_FACE = [face_of(d) for d in DIRECTIONS]
READ_FACE = [face_of(tuple(-t for t in d)) for d in DIRECTIONS]


def face_matrix():
    m = np.zeros((512, 768), np.float32)
    for face in range(6):
        axis = face // 2
        others = [i for i in range(3) if i != axis]
        for u in range(8):
            for v in range(8):
                c = [0, 0, 0]
                c[axis] = 7 if face % 2 else 0
                c[others[0]], c[others[1]] = u, v
                voxel = c[0] * 64 + c[1] * 8 + c[2]
                for half in (0, 64):
                    m[voxel, face * 128 + half + u * 8 + v] = 1
    return m


def spread_matrix(shift):
    m = np.zeros((128, 256), np.float32)
    for p in range(2):
        for y in range(8):
            for z in range(8):
                m[p * 64 + 8 * y + z, p * 128 + 10 * (y + shift) + z + shift] = 1
    return m


def ends(step):
    if step == 0:
        return [(t, t + 1) for t in range(8)]
    return [(7, 0)] if step < 0 else [(0, 9)]


YZ_GROUPS = [((0, 1, c), (0, -1, c)) for c in (-1, 0, 1)] + [((0, 0, 1), (0, 0, -1))]
X_GROUPS = [((1, b, c), (-1, b, c)) for b in (-1, 0, 1) for c in (-1, 0, 1)]


def yz_matrix():
    m = np.zeros((512, 1024), np.float32)
    for g, pair in enumerate(YZ_GROUPS):
        for h, (_, b, c) in enumerate(pair):
            for x in range(8):
                for ys, yd in ends(b):
                    for zs, zd in ends(c):
                        cell = x * 8 + (zs if b != 0 else ys)
                        m[g * 128 + h * 64 + cell, x * 128 + 10 * yd + zd] = 1
    return m


def x_matrix():
    m = np.zeros((1152, 256), np.float32)
    for g, pair in enumerate(X_GROUPS):
        for h, (a, b, c) in enumerate(pair):
            for ys, yd in ends(b):
                for zs, zd in ends(c):
                    lane = (128 if a > 0 else 0) + 10 * yd + zd
                    m[g * 128 + h * 64 + ys * 8 + zs, lane] = 1
    return m


def constant(array):
    return jnp.asarray(array, BF)


def dot(a, b):
    return lax.dot_general(a, b, (((1,), (0,)), ((), ())), preferred_element_type=F32)


def dot_nt(a, b):
    return lax.dot_general(a, b, (((1,), (1,)), ((), ())), preferred_element_type=F32)


def low_half(shape):
    return lax.broadcasted_iota(jnp.int32, shape, len(shape) - 1) < 64


def place(neighbours, place_ref, b, e):
    n = neighbours[b, e]
    mine = lax.axis_index("brick")
    owner = (n >> 2) - lax.axis_index("region") * 32
    dx = (owner & 7) - (mine & 7) + 1
    dy = (owner >> 3) - (mine >> 3) + 1
    where = jnp.where(n >= 0, dy * 3 + dx, 9)
    return n, jnp.clip(where, 0, 9)


def tables_kernel(neighbours, send_ref, index_ref, need, held, where_ref, rank_ref):
    for s in range(10):
        need[s] = 0
        held[s] = 0

    def mark(b, carry):
        for e in range(26):
            n, where = place(neighbours, None, b, e)
            where_ref[b * 26 + e] = where
            need[where] = need[where] | jnp.left_shift(1, b * 6 + SEND_FACE[e])
            held[where] = held[where] | jnp.left_shift(1, (n & 3) * 6 + READ_FACE[e])
        return carry

    lax.fori_loop(0, 4, mark, 0)
    for f in range(24):
        rank_ref[4 * 24 + f] = f
        rank_ref[9 * 24 + f] = ZERO_ROW
    for (x, y), (base, count) in ARRIVALS.items():
        s = (y + 1) * 3 + x + 1
        for t in range(8):
            send_ref[s * 8 + t] = 0
        need_bits, held_bits = need[s], held[s]

        def rank(f, carry):
            sent, got = carry
            send_ref[s * 8 + jnp.minimum(sent, 7)] = f
            rank_ref[s * 24 + f] = base + jnp.minimum(got, count - 1)
            return sent + ((need_bits >> f) & 1), got + ((held_bits >> f) & 1)

        lax.fori_loop(0, 24, rank, (0, 0), unroll=True)

    def index(b, carry):
        for e in range(26):
            n = neighbours[b, e]
            row = where_ref[b * 26 + e] * 24 + (n & 3) * 6 + READ_FACE[e]
            index_ref[b * 26 + e] = rank_ref[row]
        return carry

    lax.fori_loop(0, 4, index, 0)


def tables(neighbours):
    smem = pl.BlockSpec(memory_space=pltpu.SMEM)
    return pl.pallas_call(
        tables_kernel,
        out_shape=(
            jax.ShapeDtypeStruct((80,), jnp.int32),
            jax.ShapeDtypeStruct((104,), jnp.int32),
        ),
        in_specs=[smem],
        out_specs=(smem, smem),
        scratch_shapes=[
            pltpu.SMEM((10,), jnp.int32),
            pltpu.SMEM((10,), jnp.int32),
            pltpu.SMEM((104,), jnp.int32),
            pltpu.SMEM((240,), jnp.int32),
        ],
        name="link_tables",
    )(neighbours)


def send_slots(send_ref, x, y):
    s = (y + 1) * 3 + x + 1
    return [send_ref[s * 8 + t] for t in range(4 if y == 0 else 2)]


def pack(send_ref, tile_of, right_ref, left_ref, up_ref, down_ref):
    for ref, x in ((right_ref, 1), (left_ref, -1)):
        ids = send_slots(send_ref, x, 0) + send_slots(send_ref, x, -1) + send_slots(send_ref, x, 1)
        for t, face in enumerate(ids):
            ref[t] = tile_of(face)
    for ref, y in ((up_ref, 1), (down_ref, -1)):
        for t, face in enumerate(send_slots(send_ref, 0, y)):
            ref[t] = tile_of(face)


def first_kernel(
    send_ref, features, cotangent, active, face_mat,
    values_ref, faces_ref, right_ref, left_ref, up_ref, down_ref,
):
    for b in range(4):
        mask = active[b : b + 1, :].astype(F32)
        f = features[b].astype(F32)
        values_ref[b * 64 : b * 64 + 64, :] = (mask * (f / (1.0 + jnp.exp(-f)))).astype(BF)
        values_ref[256 + b * 64 : 320 + b * 64, :] = (mask * cotangent[b].astype(F32)).astype(BF)
    faces = dot(values_ref[...], face_mat[...]).astype(BF)
    for a in range(2):
        for b in range(4):
            for f in range(6):
                row = (a * 4 + b) * 64
                faces_ref[a, b * 6 + f] = faces[row : row + 64, f * 128 : f * 128 + 128]
    low = low_half((64, 128))
    pack(
        send_ref,
        lambda face: jnp.where(low, faces_ref[0, face], faces_ref[1, face]),
        right_ref, left_ref, up_ref, down_ref,
    )


def fill_table(table, faces, zero_too, arrays, groups):
    low = low_half((64, 128))
    for a in range(arrays):
        for f in range(24):
            table[a, f] = faces[a, f] if arrays == 2 else faces[f]
        table[a, ZERO_ROW] = jnp.zeros((64, 128), BF)
    for ref, start, base in groups:
        for t in range(start, ref.shape[0]) if start else range(4 if base < 32 else 6):
            tile = ref[t]
            if arrays == 1:
                table[0, base + t] = tile
                continue
            swapped = jnp.concatenate([tile[:, 64:], tile[:, :64]], axis=1)
            table[0, base + t] = jnp.where(low, tile, swapped)
            table[1, base + t] = jnp.where(low, swapped, tile)


def build_padded(index_ref, table, values, ext, side_yz, side_x, e_int, e_yz, e_x, arrays):
    low = low_half((64, 128))
    for a in range(arrays):
        for b in range(4):
            row = (a * 4 + b) * 64
            for side, pairs in ((side_yz, YZ_GROUPS), (side_x, X_GROUPS)):
                for g, (first, second) in enumerate(pairs):
                    lo = index_ref[b * 26 + DIRECTIONS.index(first)]
                    hi = index_ref[b * 26 + DIRECTIONS.index(second)]
                    side[row : row + 64, g * 128 : g * 128 + 128] = jnp.where(
                        low, table[a, lo], table[a, hi]
                    )
    outer = dot(side_x[...], e_x[...]).astype(BF)
    ext[:, 0:128] = outer[:, 0:128]
    ext[:, 1152:1280] = outer[:, 128:256]
    for m in range(4):
        inner = dot(values[:, m * 128 : m * 128 + 128], e_int[...])
        inner = inner + dot(side_yz[...], e_yz[:, m * 256 : m * 256 + 256])
        ext[:, 128 + m * 256 : 384 + m * 256] = inner.astype(BF)


def columns(ext, row, col):
    for p in range(10):
        plane = ext[row : row + 64, p * 128 : p * 128 + 128]
        for j in range(3):
            for l in range(3):
                s = 10 * j + l
                k = 3 * j + l
                moved = plane if s == 0 else pltpu.roll(plane, 128 - s, 1)
                col[k * 64 : k * 64 + 64, p * 128 : p * 128 + 128] = moved


def three_planes(product):
    return (
        product[0:64, 0:1024] + product[64:128, 128:1152] + product[128:192, 256:1280]
    )


def second_kernel(
    send_ref, index_ref, values, faces, from_left, from_right, from_up, from_down, active,
    w_first, w_back, gain_ref, shift_ref, face_mat, e_int, e_out, e_back, e_yz, e_x,
    hidden_ref, hidden_faces, right_ref, left_ref, up_ref, down_ref, sums_ref,
    table, ext, side_yz, side_x, col_a, col_s, stack_h, stack_s, total_h, total_s, mask_ref,
):
    groups = ((from_left, 0, 24), (from_right, 0, 28), (from_up, 0, 32), (from_down, 0, 38))
    fill_table(table, faces, True, 2, groups)
    build_padded(index_ref, table, values, ext, side_yz, side_x, e_int, e_yz, e_x, 2)
    stack_h[...] = jnp.zeros_like(stack_h)
    stack_s[...] = jnp.zeros_like(stack_s)
    on = active[...].astype(F32).astype(BF)
    for m in range(4):
        mask_ref[:, m * 256 : m * 256 + 256] = dot(on[:, m * 128 : m * 128 + 128], e_out[...])
    gain = 1.0 + gain_ref[...]
    shift = shift_ref[...]
    for b in range(4):
        columns(ext, b * 64, col_a)
        columns(ext, 256 + b * 64, col_s)
        pre = three_planes(dot(w_first[...], col_a[...]))
        back = three_planes(dot(w_back[...], col_s[...]))
        mask = mask_ref[b : b + 1, :]
        shaped = pre * gain + shift
        gate = 1.0 / (1.0 + jnp.exp(-shaped))
        hidden = (mask * (shaped * gate)).astype(BF)
        slope = (back * mask * gate * (1.0 + shaped * (1.0 - gate)) * gain).astype(BF)
        for i in range(3):
            stack_h[i * 64 : i * 64 + 64, i * 128 : i * 128 + 1024] = hidden
            stack_s[i * 64 : i * 64 + 64, i * 128 : i * 128 + 1024] = slope
        for m in range(4):
            hidden_ref[b * 64 : b * 64 + 64, m * 128 : m * 128 + 128] = dot(
                hidden[:, m * 256 : m * 256 + 256], e_back[...]
            ).astype(BF)
        part_h = dot_nt(col_s[...], stack_h[...])
        part_s = dot_nt(col_a[...], stack_s[...])
        total_h[...] = part_h if b == 0 else total_h[...] + part_h
        total_s[...] = part_s if b == 0 else total_s[...] + part_s
    for t, total in enumerate((total_h, total_s)):
        base = t * 864
        sums_ref[base : base + 576, :] = total[:, 0:128]
        sums_ref[base + 576 : base + 864, :] = jnp.concatenate(
            [total[0:288, 128:192], total[288:576, 128:192]], axis=1
        )
    sums_ref[1728:2048, :] = jnp.zeros((320, 128), F32)
    out = dot(hidden_ref[...], face_mat[...]).astype(BF)
    for b in range(4):
        for f in range(6):
            hidden_faces[b * 6 + f] = out[b * 64 : b * 64 + 64, f * 128 : f * 128 + 128]
    pack(send_ref, lambda face: hidden_faces[face], right_ref, left_ref, up_ref, down_ref)


def third_kernel(
    index_ref, hidden, hidden_faces, from_left, from_right, from_up, from_down, active, features,
    w_second, e_int, e_out, e_back, e_yz, e_x, sums,
    out_ref, first_ref, second_ref,
    table, ext, side_yz, side_x, col, mask_ref,
):
    groups = ((from_left, 0, 24), (from_right, 0, 28), (from_up, 0, 32), (from_down, 0, 38))
    fill_table(table, hidden_faces, True, 1, groups)
    build_padded(index_ref, table, hidden, ext, side_yz, side_x, e_int, e_yz, e_x, 1)
    on = active[...].astype(F32).astype(BF)
    for m in range(4):
        mask_ref[:, m * 256 : m * 256 + 256] = dot(on[:, m * 128 : m * 128 + 128], e_out[...])
    for b in range(4):
        columns(ext, b * 64, col)
        second = mask_ref[b : b + 1, :] * three_planes(dot(w_second[...], col[...]))
        for m in range(4):
            own = dot(features[b, :, m * 128 : m * 128 + 128], e_out[...])
            own = (own + second[:, m * 256 : m * 256 + 256]).astype(BF)
            out_ref[b, :, m * 128 : m * 128 + 128] = dot(own, e_back[...]).astype(BF)
    for t in range(2):
        base = t * 864
        for i in range(3):
            for jl in range(9):
                if i < 2:
                    block = sums[base + jl * 64 : base + jl * 64 + 64, i * 64 : i * 64 + 64]
                else:
                    pieces = []
                    for r in (jl * 64, jl * 64 + 32):
                        lane, at = (0, r) if r < 288 else (64, r - 288)
                        at += base + 576
                        pieces.append(sums[at : at + 32, lane : lane + 64])
                    block = jnp.concatenate(pieces, axis=0)
                k = 9 * i + jl
                if t == 0:
                    second_ref[26 - k] = block
                else:
                    first_ref[k] = block.T


def sent(array, step):
    pairs = []
    for i in range(32):
        j = i + step
        if 0 <= j < 32 and (abs(step) == GRID_X or i // GRID_X == j // GRID_X):
            pairs.append((i, j))
    return lax.ppermute(array, "brick", pairs)


def exchange(right, left, up, down):
    from_left = sent(right, 1)
    from_right = sent(left, -1)
    from_up = sent(jnp.concatenate([up, from_left[6:8], from_right[6:8]], axis=0), GRID_X)
    from_down = sent(jnp.concatenate([down, from_left[4:6], from_right[4:6]], axis=0), -GRID_X)
    return from_left, from_right, from_up, from_down


def stacked(weight):
    return weight.reshape(3, 9, 64, 64).transpose(0, 2, 1, 3).reshape(192, 576)


def shape(dims, dtype=BF):
    return jax.ShapeDtypeStruct(dims, dtype)


def call(kernel, outs, scratch, prefetch, *operands):
    smem = pl.BlockSpec(memory_space=pltpu.SMEM)
    vmem = pl.BlockSpec(memory_space=pltpu.VMEM)
    return pl.pallas_call(
        kernel,
        out_shape=tuple(outs),
        in_specs=[smem] * prefetch + [vmem] * (len(operands) - prefetch),
        out_specs=tuple(vmem for _ in outs),
        scratch_shapes=scratch,
        compiler_params=pltpu.CompilerParams(vmem_limit_bytes=VMEM_LIMIT),
        name=kernel.__name__,
    )(*operands)


def shards(
    features, active, neighbours, first_weight, second_weight, film_scale, film_shift, cotangent
):
    face_mat = constant(face_matrix())
    e_int, e_out = constant(spread_matrix(1)), constant(spread_matrix(0))
    e_back = constant(spread_matrix(0).T)
    e_yz, e_x = constant(yz_matrix()), constant(x_matrix())
    messages = [shape((8, 64, 128)), shape((8, 64, 128)), shape((2, 64, 128)), shape((2, 64, 128))]

    send_ids, index = tables(neighbours)
    values, faces, *outgoing = call(
        first_kernel,
        [shape((512, 512)), shape((2, 24, 64, 128))] + messages,
        [],
        1,
        send_ids, features, cotangent, active, face_mat,
    )
    arrived = exchange(*outgoing)
    w_first = stacked(first_weight)
    w_second = stacked(second_weight)
    w_back = stacked(second_weight[::-1].transpose(0, 2, 1))

    hidden, hidden_faces, *outgoing, sums = call(
        second_kernel,
        [shape((256, 512)), shape((24, 64, 128))] + messages + [shape((2048, 128), F32)],
        [
            pltpu.VMEM((2, 45, 64, 128), BF),
            pltpu.VMEM((512, 1280), BF),
            pltpu.VMEM((512, 512), BF),
            pltpu.VMEM((512, 1152), BF),
            pltpu.VMEM((576, 1280), BF),
            pltpu.VMEM((576, 1280), BF),
            pltpu.VMEM((192, 1280), BF),
            pltpu.VMEM((192, 1280), BF),
            pltpu.VMEM((576, 192), F32),
            pltpu.VMEM((576, 192), F32),
            pltpu.VMEM((4, 1024), F32),
        ],
        2,
        send_ids, index, values, faces, *arrived, active, w_first, w_back,
        film_scale.reshape(64, 1), film_shift.reshape(64, 1),
        face_mat, e_int, e_out, e_back, e_yz, e_x,
    )
    arrived = exchange(*outgoing)
    parts = lax.all_to_all(sums.reshape(128, 16, 128), AXES, 0, 0, tiled=True)
    mine = jnp.sum(parts, axis=0)
    sums = lax.all_to_all(jnp.broadcast_to(mine, (128, 16, 128)), AXES, 0, 0, tiled=True)
    block_output, grad_first, grad_second = call(
        third_kernel,
        [shape((4, 64, 512)), shape((27, 64, 64), F32), shape((27, 64, 64), F32)],
        [
            pltpu.VMEM((1, 45, 64, 128), BF),
            pltpu.VMEM((256, 1280), BF),
            pltpu.VMEM((256, 512), BF),
            pltpu.VMEM((256, 1152), BF),
            pltpu.VMEM((576, 1280), BF),
            pltpu.VMEM((4, 1024), F32),
        ],
        1,
        index, hidden, hidden_faces, *arrived, active, features, w_second,
        e_int, e_out, e_back, e_yz, e_x, sums.reshape(2048, 128),
    )
    return block_output, grad_first, grad_second


def solution(mesh):
    split = P(AXES, None, None)
    rows = P(AXES, None)
    return jax.shard_map(
        shards,
        mesh=mesh,
        in_specs=(split, rows, rows, P(), P(), P(), P(), split),
        out_specs=(split, P(), P()),
        check_vma=False,
    )
```

```python
import jax
import jax.numpy as jnp
from jax import lax
from jax.experimental import pallas as pl
from jax.experimental.pallas import tpu as pltpu
from jax.sharding import PartitionSpec as P

AXES = ("region", "brick")
GRID_X = 8
ZERO_ROW = 44
ARRIVALS = {
    (-1, 0): (24, 4),
    (1, 0): (28, 4),
    (0, -1): (32, 2),
    (-1, -1): (34, 2),
    (1, -1): (36, 2),
    (0, 1): (38, 2),
    (-1, 1): (40, 2),
    (1, 1): (42, 2),
}
BF = jnp.bfloat16
F32 = jnp.float32


def direction_list():
    return [
        (a, b, c)
        for a in (-1, 0, 1)
        for b in (-1, 0, 1)
        for c in (-1, 0, 1)
        if (a, b, c) != (0, 0, 0)
    ]


DIRECTIONS = direction_list()


def face_of(vector):
    if vector[0] != 0:
        return 0 if vector[0] < 0 else 1
    if vector[1] != 0:
        return 2 if vector[1] < 0 else 3
    return 4 if vector[2] < 0 else 5


SEND_FACE = [face_of(d) for d in DIRECTIONS]
READ_FACE = [face_of(tuple(-t for t in d)) for d in DIRECTIONS]


YZ_GROUPS = [((0, 1, c), (0, -1, c)) for c in (-1, 0, 1)] + [((0, 0, 1), (0, 0, -1))]
X_GROUPS = [((1, b, c), (-1, b, c)) for b in (-1, 0, 1) for c in (-1, 0, 1)]


def one_hot(rows, source):
    at = lax.broadcasted_iota(jnp.int32, (rows, source.shape[1]), 0)
    return jnp.where(at == source, 1.0, 0.0).astype(BF)


def lanes(count):
    return lax.broadcasted_iota(jnp.int32, (1, count), 1)


def face_matrix():
    lane = lanes(768)
    face, u, v = lane >> 7, (lane >> 3) & 7, lane & 7
    first = jnp.where(face < 2, u * 8 + v, jnp.where(face < 4, u * 64 + v, u * 64 + v * 8))
    far = jnp.where(face == 1, 448, jnp.where(face == 3, 56, jnp.where(face == 5, 7, 0)))
    return one_hot(512, first + far)


def padded_lane(count):
    lane = lanes(count)
    cell = lane & 127
    y = (cell * 205) >> 11
    return lane >> 7, y, cell - y * 10


def spread_matrix(shift):
    plane, y, z = padded_lane(256)
    y, z = y - shift, z - shift
    inside = (y >= 0) & (y < 8) & (z >= 0) & (z < 8)
    return one_hot(128, jnp.where(inside, plane * 64 + y * 8 + z, -1))


def yz_matrix():
    x, y, z = padded_lane(1024)
    group = jnp.where(z == 0, 0, jnp.where(z == 9, 2, 1))
    y_edge, z_edge = (y == 0) | (y == 9), (z == 0) | (z == 9)
    z_cell = jnp.where(z == 0, 7, jnp.where(z == 9, 0, z - 1))
    from_y = group * 128 + jnp.where(y == 0, 64, 0) + x * 8 + z_cell
    from_z = 384 + jnp.where(z == 0, 64, 0) + x * 8 + y - 1
    source = jnp.where(y_edge, from_y, jnp.where(z_edge & (y < 9), from_z, -1))
    return one_hot(512, source)


def x_matrix():
    side, y, z = padded_lane(256)
    y_group = jnp.where(y == 0, 0, jnp.where(y == 9, 2, 1))
    z_group = jnp.where(z == 0, 0, jnp.where(z == 9, 2, 1))
    y_cell = jnp.where(y == 0, 7, jnp.where(y == 9, 0, y - 1))
    z_cell = jnp.where(z == 0, 7, jnp.where(z == 9, 0, z - 1))
    source = (y_group * 3 + z_group) * 128 + jnp.where(side == 0, 64, 0) + y_cell * 8 + z_cell
    return one_hot(1152, jnp.where(y < 10, source, -1))


def dot(a, b):
    return lax.dot_general(a, b, (((1,), (0,)), ((), ())), preferred_element_type=F32)


def dot_nt(a, b):
    return lax.dot_general(a, b, (((1,), (1,)), ((), ())), preferred_element_type=F32)


def low_half(shape):
    return lax.broadcasted_iota(jnp.int32, shape, len(shape) - 1) < 64


def place(n):
    mine = lax.axis_index("brick")
    owner = (n >> 2) - lax.axis_index("region") * 32
    dx = (owner & 7) - (mine & 7) + 1
    dy = (owner >> 3) - (mine >> 3) + 1
    return jnp.where(n >= 0, jnp.clip(dy * 3 + dx, 0, 8), 9)


def choose_sends(neighbours, send_ref):
    readers = []
    for b in range(4):
        for f in range(6):
            bits = 0
            for e in range(26):
                if SEND_FACE[e] == f:
                    bits = bits | jnp.left_shift(1, place(neighbours[b, e]))
            readers.append(bits)
    for x, y in ARRIVALS:
        s = (y + 1) * 3 + x + 1
        for t in range(8):
            send_ref[s * 8 + t] = 0
        sent = 0
        for f in range(24):
            send_ref[s * 8 + jnp.minimum(sent, 7)] = f
            sent = sent + ((readers[f] >> s) & 1)


def tables_kernel(neighbours_any, after_any, index_ref, neighbours, held, where_ref, rank_ref, sem):
    copy = pltpu.make_async_copy(neighbours_any, neighbours, sem)
    copy.start()
    copy.wait()
    for s in range(10):
        held[s] = 0

    def mark(b, carry):
        for e in range(26):
            n = neighbours[b, e]
            where = place(n)
            where_ref[b * 26 + e] = where
            held[where] = held[where] | jnp.left_shift(1, (n & 3) * 6 + READ_FACE[e])
        return carry

    lax.fori_loop(0, 4, mark, 0)
    for f in range(24):
        rank_ref[4 * 24 + f] = f
        rank_ref[9 * 24 + f] = ZERO_ROW
    for (x, y), (base, count) in ARRIVALS.items():
        s = (y + 1) * 3 + x + 1
        bits = held[s]
        got = 0
        for f in range(24):
            rank_ref[s * 24 + f] = base + jnp.minimum(got, count - 1)
            got = got + ((bits >> f) & 1)

    def index(b, carry):
        for e in range(26):
            row = where_ref[b * 26 + e] * 24 + (neighbours[b, e] & 3) * 6 + READ_FACE[e]
            index_ref[b * 26 + e] = rank_ref[row]
        return carry

    lax.fori_loop(0, 4, index, 0)


def send_slots(send_ref, x, y):
    s = (y + 1) * 3 + x + 1
    return [send_ref[s * 8 + t] for t in range(4 if y == 0 else 2)]


def pack(send_ref, tiles_of, right_ref, left_ref, up_ref, down_ref):
    for ref, x in ((right_ref, 1), (left_ref, -1)):
        ids = send_slots(send_ref, x, 0) + send_slots(send_ref, x, -1) + send_slots(send_ref, x, 1)
        for t, tile in enumerate(tiles_of(ids)):
            ref[t] = tile
    for ref, y in ((up_ref, 1), (down_ref, -1)):
        for t, tile in enumerate(tiles_of(send_slots(send_ref, 0, y))):
            ref[t] = tile


def first_kernel(
    neighbours_any, features_any, cotangent_any, active_any,
    values_ref, faces_ref, right_ref, left_ref, up_ref, down_ref, send_ref, active,
    neighbours, features, cotangent, sems,
):
    pairs = (
        (neighbours_any, neighbours), (features_any, features), (cotangent_any, cotangent),
        (active_any, active),
    )
    copies = [pltpu.make_async_copy(s, d, sems.at[t]) for t, (s, d) in enumerate(pairs)]
    for copy in copies:
        copy.start()
    copies[0].wait()
    choose_sends(neighbours, send_ref)
    for copy in copies[1:]:
        copy.wait()
    for b in range(4):
        mask = active[b : b + 1, :].astype(F32)
        f = features[b].astype(F32)
        values_ref[b * 64 : b * 64 + 64, :] = (mask * (f / (1.0 + jnp.exp(-f)))).astype(BF)
        values_ref[256 + b * 64 : 320 + b * 64, :] = (mask * cotangent[b].astype(F32)).astype(BF)
    faces = dot(values_ref[...], face_matrix()).astype(BF)
    for a in range(2):
        for b in range(4):
            for f in range(6):
                row = (a * 4 + b) * 64
                faces_ref[a, b * 6 + f] = faces[row : row + 64, f * 128 : f * 128 + 128]
    low = low_half((64, 128))
    pack(
        send_ref,
        lambda ids: [jnp.where(low, faces_ref[0, i], faces_ref[1, i]) for i in ids],
        right_ref, left_ref, up_ref, down_ref,
    )


def as_column(row):
    here = lax.broadcasted_iota(jnp.int32, (64, 64), 0)
    there = lax.broadcasted_iota(jnp.int32, (64, 64), 1)
    picked = jnp.where(here == there, jnp.broadcast_to(row, (64, 64)), 0.0)
    return jnp.broadcast_to(jnp.sum(picked, axis=1, keepdims=True), (64, 128))


def prepare_kernel(
    first, second, scale, shift,
    w_first, w_back, gain_ref, shift_ref, e_int, e_out, e_yz, e_x,
):
    e_int[...], e_out[...] = spread_matrix(1), spread_matrix(0)
    e_yz[...], e_x[...] = yz_matrix(), x_matrix()
    gain_ref[...] = 1.0 + as_column(scale[...])
    shift_ref[...] = as_column(shift[...])
    for i in range(3):
        for jl in range(9):
            k = 9 * i + jl
            rows, lanes = slice(i * 64, i * 64 + 64), slice(jl * 64, jl * 64 + 64)
            w_first[rows, lanes] = first[k]
            w_back[rows, lanes] = second[26 - k].T


def fill_table(table, faces, arrays, groups):
    low = low_half((64, 128))
    for a in range(arrays):
        for f in range(24):
            table[a, f] = faces[a, f] if arrays == 2 else faces[f]
        table[a, ZERO_ROW] = jnp.zeros((64, 128), BF)
    for ref, base, count in groups:
        for t in range(count * arrays // 2):
            tile = ref[t]
            swapped = jnp.concatenate([tile[:, 64:], tile[:, :64]], axis=1)
            first, second = jnp.where(low, tile, swapped), jnp.where(low, swapped, tile)
            if arrays == 2:
                table[0, base + t], table[1, base + t] = first, second
            else:
                table[0, base + 2 * t], table[0, base + 2 * t + 1] = first, second


def build_padded(index_ref, table, values, ext, side_yz, side_x, e_int, e_yz, e_x, arrays):
    low = low_half((64, 128))
    for a in range(arrays):
        for b in range(4):
            row = (a * 4 + b) * 64
            for side, pairs in ((side_yz, YZ_GROUPS), (side_x, X_GROUPS)):
                for g, (first, second) in enumerate(pairs):
                    lo = index_ref[b * 26 + DIRECTIONS.index(first)]
                    hi = index_ref[b * 26 + DIRECTIONS.index(second)]
                    side[row : row + 64, g * 128 : g * 128 + 128] = jnp.where(
                        low, table[a, lo], table[a, hi]
                    )
    outer = dot(side_x[...], e_x[...]).astype(BF)
    ext[:, 0:128] = outer[:, 0:128]
    ext[:, 1152:1280] = outer[:, 128:256]
    for m in range(4):
        inner = dot(values[:, m * 128 : m * 128 + 128], e_int[...])
        inner = inner + dot(side_yz[...], e_yz[:, m * 256 : m * 256 + 256])
        ext[:, 128 + m * 256 : 384 + m * 256] = inner.astype(BF)


def columns(ext, row, col):
    for p in range(10):
        plane = ext[row : row + 64, p * 128 : p * 128 + 128]
        for j in range(3):
            for l in range(3):
                s = 10 * j + l
                k = 3 * j + l
                moved = plane if s == 0 else pltpu.roll(plane, 128 - s, 1)
                col[k * 64 : k * 64 + 64, p * 128 : p * 128 + 128] = moved


def three_planes(product):
    return (
        product[0:64, 0:1024] + product[64:128, 128:1152] + product[128:192, 256:1280]
    )


def second_kernel(
    index_ref, values, faces, from_left, from_right, from_up, from_down, active,
    w_first, w_back, gain_ref, shift_ref, e_int, e_out, e_yz, e_x,
    hidden_ref, sums_ref, mask_ref,
    table, ext, side_yz, side_x, col_a, col_s, stack_h, stack_s, total_h, total_s,
):
    groups = ((from_left, 24, 4), (from_right, 28, 4), (from_up, 32, 6), (from_down, 38, 6))
    fill_table(table, faces, 2, groups)
    build_padded(index_ref, table, values, ext, side_yz, side_x, e_int, e_yz, e_x, 2)
    stack_h[...] = jnp.zeros_like(stack_h)
    stack_s[...] = jnp.zeros_like(stack_s)
    on = active[...].astype(F32).astype(BF)
    for m in range(4):
        mask_ref[:, m * 256 : m * 256 + 256] = dot(on[:, m * 128 : m * 128 + 128], e_out[...])
    gain = gain_ref[:, 0:1]
    shift = shift_ref[:, 0:1]
    for b in range(4):
        columns(ext, b * 64, col_a)
        columns(ext, 256 + b * 64, col_s)
        pre = three_planes(dot(w_first[...], col_a[...]))
        back = three_planes(dot(w_back[...], col_s[...]))
        mask = mask_ref[b : b + 1, :]
        shaped = pre * gain + shift
        gate = 1.0 / (1.0 + jnp.exp(-shaped))
        hidden = (mask * (shaped * gate)).astype(BF)
        slope = (back * mask * gate * (1.0 + shaped * (1.0 - gate)) * gain).astype(BF)
        for i in range(3):
            stack_h[i * 64 : i * 64 + 64, i * 128 : i * 128 + 1024] = hidden
            stack_s[i * 64 : i * 64 + 64, i * 128 : i * 128 + 1024] = slope
        for m in range(4):
            hidden_ref[b * 64 : b * 64 + 64, m * 128 : m * 128 + 128] = dot_nt(
                hidden[:, m * 256 : m * 256 + 256], e_out[...]
            ).astype(BF)
        part_h = dot_nt(col_s[...], stack_h[...])
        part_s = dot_nt(col_a[...], stack_s[...])
        total_h[...] = part_h if b == 0 else total_h[...] + part_h
        total_s[...] = part_s if b == 0 else total_s[...] + part_s
    pack_sums(total_h, total_s, sums_ref)


def faces_kernel(
    send_ref, hidden,
    hidden_faces, right_ref, left_ref, up_ref, down_ref,
):
    out = dot(hidden[...], face_matrix()).astype(BF)
    for b in range(4):
        for f in range(6):
            hidden_faces[b * 6 + f] = out[b * 64 : b * 64 + 64, f * 128 : f * 128 + 128]
    low = low_half((64, 128))
    pack(
        send_ref,
        lambda ids: [
            jnp.where(low, hidden_faces[i], hidden_faces[j]) for i, j in zip(ids[::2], ids[1::2])
        ],
        right_ref, left_ref, up_ref, down_ref,
    )


def pack_sums(total_h, total_s, sums_ref):
    for t, total in enumerate((total_h, total_s)):
        base = t * 864
        sums_ref[base : base + 576, :] = total[:, 0:128].astype(BF)
        sums_ref[base + 576 : base + 864, :] = jnp.concatenate(
            [total[0:288, 128:192], total[288:576, 128:192]], axis=1
        ).astype(BF)
    sums_ref[1728:2048, :] = jnp.zeros((320, 128), BF)


def third_kernel(
    index_ref, hidden_faces, from_left, from_right, from_up, from_down, mask_ref,
    hidden, features, weight,
    out_ref,
    table, ext, side_yz, side_x, col, w_second, e_int, e_out, e_yz, e_x,
):
    e_int[...], e_out[...] = spread_matrix(1), spread_matrix(0)
    e_yz[...], e_x[...] = yz_matrix(), x_matrix()
    for i in range(3):
        for jl in range(9):
            w_second[i * 64 : i * 64 + 64, jl * 64 : jl * 64 + 64] = weight[9 * i + jl]
    groups = ((from_left, 24, 4), (from_right, 28, 4), (from_up, 32, 6), (from_down, 38, 6))
    fill_table(table, hidden_faces, 1, groups)
    build_padded(index_ref, table, hidden, ext, side_yz, side_x, e_int, e_yz, e_x, 1)
    for b in range(4):
        columns(ext, b * 64, col)
        second = mask_ref[b : b + 1, :] * three_planes(dot(w_second[...], col[...]))
        for m in range(4):
            own = dot(features[b, :, m * 128 : m * 128 + 128], e_out[...])
            own = (own + second[:, m * 256 : m * 256 + 256]).astype(BF)
            out_ref[b, :, m * 128 : m * 128 + 128] = dot_nt(own, e_out[...]).astype(BF)


def share_kernel(parts, left_any, right_any, out_ref):
    total = parts[0].astype(F32)
    for d in range(1, 128):
        total = total + parts[d].astype(F32)
    total = total.astype(BF)
    for d in range(128):
        out_ref[d] = total


def unpack_kernel(sums, first_ref, second_ref):
    for t in range(2):
        base = t * 864
        for i in range(3):
            for jl in range(9):
                if i < 2:
                    block = sums[base + jl * 64 : base + jl * 64 + 64, i * 64 : i * 64 + 64]
                else:
                    pieces = []
                    for r in (jl * 64, jl * 64 + 32):
                        lane, at = (0, r) if r < 288 else (64, r - 288)
                        at += base + 576
                        pieces.append(sums[at : at + 32, lane : lane + 64])
                    block = jnp.concatenate(pieces, axis=0)
                block = block.astype(F32)
                k = 9 * i + jl
                if t == 0:
                    second_ref[26 - k] = block
                else:
                    first_ref[k] = block.T


def sent(array, step):
    pairs = []
    for i in range(32):
        j = i + step
        if 0 <= j < 32 and (abs(step) == GRID_X or i // GRID_X == j // GRID_X):
            pairs.append((i, j))
    return lax.ppermute(array, "brick", pairs)


def forward_kernel(from_left, from_right, up, down, after_any, up_ref, down_ref):
    n = up.shape[0]
    up_ref[0:n] = up[...]
    down_ref[0:n] = down[...]
    for t, ref in enumerate((from_left, from_right)):
        up_ref[n + t * n : 2 * n + t * n] = ref[3 * n :]
        down_ref[n + t * n : 2 * n + t * n] = ref[2 * n : 3 * n]


def first_round(right, left):
    return sent(right, 1), sent(left, -1)


def second_round(from_left, from_right, up, down, after):
    upward, downward = call(
        forward_kernel,
        [(VMEM, t) for t in (from_left, from_right, up, down)] + [(ANY, after)],
        [(VMEM, shape((3 * up.shape[0], 64, 128)))] * 2,
        [],
        8,
        0,
    )
    return from_left, from_right, sent(upward, GRID_X), sent(downward, -GRID_X)


def shape(dims, dtype=BF):
    return jax.ShapeDtypeStruct(dims, dtype)


SMEM = pl.BlockSpec(memory_space=pltpu.SMEM)
VMEM = pl.BlockSpec(memory_space=pltpu.VMEM)
ANY = pl.BlockSpec(memory_space=pl.ANY)
HBM = pl.BlockSpec(memory_space=pltpu.HBM)


def call(kernel, operands, outs, scratch, limit, us):
    return pl.pallas_call(
        kernel,
        out_shape=tuple(o for _, o in outs),
        in_specs=[s for s, _ in operands],
        out_specs=tuple(s for s, _ in outs),
        scratch_shapes=scratch,
        compiler_params=pltpu.CompilerParams(vmem_limit_bytes=limit << 20),
        cost_estimate=pl.CostEstimate(flops=us * 10**9, bytes_accessed=0, transcendentals=0),
        name=kernel.__name__,
    )(*(o for _, o in operands))


def shards(
    features, active, neighbours, first_weight, second_weight, film_scale, film_shift, cotangent
):
    def messages(arrays):
        return [(VMEM, shape((n * arrays, 64, 128))) for n in (4, 4, 1, 1)]


    values, faces, *outgoing, send_ids, on = call(
        first_kernel,
        [(HBM, t) for t in (neighbours, features, cotangent, active)],
        [(VMEM, shape((512, 512))), (VMEM, shape((2, 24, 64, 128)))]
        + messages(2)
        + [(SMEM, shape((80,), jnp.int32)), (VMEM, shape((4, 512), jnp.int32))],
        [
            pltpu.SMEM((4, 26), jnp.int32),
            pltpu.VMEM((4, 64, 512), BF),
            pltpu.VMEM((4, 64, 512), BF),
            pltpu.SemaphoreType.DMA((4,)),
        ],
        58,
        4,
    )
    arrived = second_round(*first_round(*outgoing[:2]), *outgoing[2:], neighbours)
    (index,) = call(
        tables_kernel,
        [(HBM, neighbours), (ANY, arrived[0])],
        [(SMEM, shape((104,), jnp.int32))],
        [
            pltpu.SMEM((4, 26), jnp.int32),
            pltpu.SMEM((10,), jnp.int32),
            pltpu.SMEM((104,), jnp.int32),
            pltpu.SMEM((240,), jnp.int32),
            pltpu.SemaphoreType.DMA,
        ],
        8,
        3,
    )
    spread_shapes = [(128, 256), (128, 256), (512, 1024), (1152, 256)]
    prepared = call(
        prepare_kernel,
        [
            (VMEM, t)
            for t in (
                first_weight,
                second_weight,
                film_scale.reshape(1, 64),
                film_shift.reshape(1, 64),
            )
        ],
        [(VMEM, shape((192, 576)))] * 2
        + [(VMEM, shape((64, 128), F32))] * 2
        + [(VMEM, shape(dims)) for dims in spread_shapes],
        [],
        16,
        3,
    )
    w_first, w_back, gain, shift, *spreads = prepared

    hidden, sums, mask = call(
        second_kernel,
        [(SMEM, index)]
        + [(VMEM, t) for t in (values, faces, *arrived, on, w_first, w_back, gain, shift)]
        + [(VMEM, t) for t in spreads],
        [
            (VMEM, shape((256, 512))),
            (VMEM, shape((2048, 128))),
            (VMEM, shape((4, 1024), F32)),
        ],
        [
            pltpu.VMEM((2, 45, 64, 128), BF),
            pltpu.VMEM((512, 1280), BF),
            pltpu.VMEM((512, 512), BF),
            pltpu.VMEM((512, 1152), BF),
            pltpu.VMEM((576, 1280), BF),
            pltpu.VMEM((576, 1280), BF),
            pltpu.VMEM((192, 1280), BF),
            pltpu.VMEM((192, 1280), BF),
            pltpu.VMEM((576, 192), F32),
            pltpu.VMEM((576, 192), F32),
        ],
        24,
        10,
    )
    parts = lax.all_to_all(sums.reshape(128, 16, 128), AXES, 0, 0, tiled=True)
    hidden_faces, *outgoing = call(
        faces_kernel,
        [(SMEM, send_ids), (VMEM, hidden)],
        [(VMEM, shape((24, 64, 128)))] + messages(1),
        [],
        16,
        8,
    )
    sides = first_round(*outgoing[:2])
    (shares,) = call(
        share_kernel, [(VMEM, parts)] + [(ANY, t) for t in sides], [(VMEM, shape((128, 16, 128)))], [], 16, 1
    )
    arrived = second_round(*sides, *outgoing[2:], shares)
    sums = lax.all_to_all(shares, AXES, 0, 0, tiled=True)
    (block_output,) = call(
        third_kernel,
        [(SMEM, index)]
        + [(VMEM, t) for t in (hidden_faces, *arrived, mask, hidden, features, second_weight)],
        [(VMEM, shape((4, 64, 512)))],
        [
            pltpu.VMEM((1, 45, 64, 128), BF),
            pltpu.VMEM((256, 1280), BF),
            pltpu.VMEM((256, 512), BF),
            pltpu.VMEM((256, 1152), BF),
            pltpu.VMEM((576, 1280), BF),
            pltpu.VMEM((192, 576), BF),
        ]
        + [pltpu.VMEM(dims, BF) for dims in spread_shapes],
        16,
        2,
    )
    grad_first, grad_second = call(
        unpack_kernel,
        [(VMEM, sums.reshape(2048, 128))],
        [(VMEM, shape((27, 64, 64), F32))] * 2,
        [],
        16,
        0,
    )
    return block_output, grad_first, grad_second


def solution(mesh):
    split = P(AXES, None, None)
    rows = P(AXES, None)
    return jax.shard_map(
        shards,
        mesh=mesh,
        in_specs=(split, rows, rows, P(), P(), P(), P(), split),
        out_specs=(split, P(), P()),
        check_vma=False,
    )
```

```python
import jax
import jax.numpy as jnp
from jax import lax
from jax.experimental import pallas as pl
from jax.experimental.pallas import tpu as pltpu
from jax.sharding import PartitionSpec as P

AXES = ("region", "brick")
GRID_X = 8
ZERO_ROW = 44
ARRIVALS = {
    (-1, 0): (24, 4),
    (1, 0): (28, 4),
    (0, -1): (32, 2),
    (-1, -1): (34, 2),
    (1, -1): (36, 2),
    (0, 1): (38, 2),
    (-1, 1): (40, 2),
    (1, 1): (42, 2),
}
BF = jnp.bfloat16
F32 = jnp.float32


def direction_list():
    return [
        (a, b, c)
        for a in (-1, 0, 1)
        for b in (-1, 0, 1)
        for c in (-1, 0, 1)
        if (a, b, c) != (0, 0, 0)
    ]


DIRECTIONS = direction_list()


def face_of(vector):
    if vector[0] != 0:
        return 0 if vector[0] < 0 else 1
    if vector[1] != 0:
        return 2 if vector[1] < 0 else 3
    return 4 if vector[2] < 0 else 5


SEND_FACE = [face_of(d) for d in DIRECTIONS]
READ_FACE = [face_of(tuple(-t for t in d)) for d in DIRECTIONS]


YZ_GROUPS = [((0, 1, c), (0, -1, c)) for c in (-1, 0, 1)] + [((0, 0, 1), (0, 0, -1))]
X_GROUPS = [((1, b, c), (-1, b, c)) for b in (-1, 0, 1) for c in (-1, 0, 1)]


def one_hot(rows, source):
    at = lax.broadcasted_iota(jnp.int32, (rows, source.shape[1]), 0)
    return jnp.where(at == source, 1.0, 0.0).astype(BF)


def lanes(count):
    return lax.broadcasted_iota(jnp.int32, (1, count), 1)


def face_matrix():
    lane = lanes(768)
    face, u, v = lane >> 7, (lane >> 3) & 7, lane & 7
    first = jnp.where(face < 2, u * 8 + v, jnp.where(face < 4, u * 64 + v, u * 64 + v * 8))
    far = jnp.where(face == 1, 448, jnp.where(face == 3, 56, jnp.where(face == 5, 7, 0)))
    return one_hot(512, first + far)


def padded_lane(count):
    lane = lanes(count)
    cell = lane & 127
    y = (cell * 205) >> 11
    return lane >> 7, y, cell - y * 10


def spread_matrix():
    plane, y, z = padded_lane(256)
    y, z = y - 1, z - 1
    inside = (y >= 0) & (y < 8) & (z >= 0) & (z < 8)
    return one_hot(128, jnp.where(inside, plane * 64 + y * 8 + z, -1))


def window_matrix():
    lane = lanes(1152)
    tap, plane, y, z = lane >> 7, (lane >> 6) & 1, (lane >> 3) & 7, lane & 7
    j = jnp.where(tap < 3, 0, jnp.where(tap < 6, 1, 2))
    return one_hot(256, plane * 128 + (y + j) * 10 + z + tap - 3 * j)


def yz_matrix():
    x, y, z = padded_lane(1024)
    group = jnp.where(z == 0, 0, jnp.where(z == 9, 2, 1))
    y_edge, z_edge = (y == 0) | (y == 9), (z == 0) | (z == 9)
    z_cell = jnp.where(z == 0, 7, jnp.where(z == 9, 0, z - 1))
    from_y = group * 128 + jnp.where(y == 0, 64, 0) + x * 8 + z_cell
    from_z = 384 + jnp.where(z == 0, 64, 0) + x * 8 + y - 1
    source = jnp.where(y_edge, from_y, jnp.where(z_edge & (y < 9), from_z, -1))
    return one_hot(512, source)


def x_matrix():
    side, y, z = padded_lane(256)
    y_group = jnp.where(y == 0, 0, jnp.where(y == 9, 2, 1))
    z_group = jnp.where(z == 0, 0, jnp.where(z == 9, 2, 1))
    y_cell = jnp.where(y == 0, 7, jnp.where(y == 9, 0, y - 1))
    z_cell = jnp.where(z == 0, 7, jnp.where(z == 9, 0, z - 1))
    source = (y_group * 3 + z_group) * 128 + jnp.where(side == 0, 64, 0) + y_cell * 8 + z_cell
    return one_hot(1152, jnp.where(y < 10, source, -1))


def dot(a, b):
    return lax.dot_general(a, b, (((1,), (0,)), ((), ())), preferred_element_type=F32)


def dot_nt(a, b):
    return lax.dot_general(a, b, (((1,), (1,)), ((), ())), preferred_element_type=F32)


def low_half(shape):
    return lax.broadcasted_iota(jnp.int32, shape, len(shape) - 1) < 64


def place(n):
    mine = lax.axis_index("brick")
    owner = (n >> 2) - lax.axis_index("region") * 32
    dx = (owner & 7) - (mine & 7) + 1
    dy = (owner >> 3) - (mine >> 3) + 1
    return jnp.where(n >= 0, jnp.clip(dy * 3 + dx, 0, 8), 9)


def choose_sends(neighbours, send_ref):
    readers = []
    for b in range(4):
        for f in range(6):
            bits = 0
            for e in range(26):
                if SEND_FACE[e] == f:
                    bits = bits | jnp.left_shift(1, place(neighbours[b, e]))
            readers.append(bits)
    for x, y in ARRIVALS:
        s = (y + 1) * 3 + x + 1
        for t in range(8):
            send_ref[s * 8 + t] = 0
        sent = 0
        for f in range(24):
            send_ref[s * 8 + jnp.minimum(sent, 7)] = f
            sent = sent + ((readers[f] >> s) & 1)


def tables_kernel(
    neighbours_any, after_any, index_ref, send_ref, neighbours, held, where_ref, rank_ref, sem
):
    copy = pltpu.make_async_copy(neighbours_any, neighbours, sem)
    copy.start()
    copy.wait()
    choose_sends(neighbours, send_ref)
    for s in range(10):
        held[s] = 0

    def mark(b, carry):
        for e in range(26):
            n = neighbours[b, e]
            where = place(n)
            where_ref[b * 26 + e] = where
            held[where] = held[where] | jnp.left_shift(1, (n & 3) * 6 + READ_FACE[e])
        return carry

    lax.fori_loop(0, 4, mark, 0)
    for f in range(24):
        rank_ref[4 * 24 + f] = f
        rank_ref[9 * 24 + f] = ZERO_ROW
    for (x, y), (base, count) in ARRIVALS.items():
        s = (y + 1) * 3 + x + 1
        bits = held[s]
        got = 0
        for f in range(24):
            rank_ref[s * 24 + f] = base + jnp.minimum(got, count - 1)
            got = got + ((bits >> f) & 1)

    def index(b, carry):
        for e in range(26):
            row = where_ref[b * 26 + e] * 24 + (neighbours[b, e] & 3) * 6 + READ_FACE[e]
            index_ref[b * 26 + e] = rank_ref[row]
        return carry

    lax.fori_loop(0, 4, index, 0)


def send_slots(send_ref, x, y):
    s = (y + 1) * 3 + x + 1
    return [send_ref[s * 8 + t] for t in range(4 if y == 0 else 2)]


def pack(send_ref, tiles_of, right_ref, left_ref, up_ref, down_ref):
    for ref, x in ((right_ref, 1), (left_ref, -1)):
        ids = send_slots(send_ref, x, 0) + send_slots(send_ref, x, -1) + send_slots(send_ref, x, 1)
        for t, tile in enumerate(tiles_of(ids)):
            ref[t] = tile
    for ref, y in ((up_ref, 1), (down_ref, -1)):
        for t, tile in enumerate(tiles_of(send_slots(send_ref, 0, y))):
            ref[t] = tile


def first_kernel(
    neighbours_any, features_any, cotangent_any, active_any,
    values_ref, faces_ref, right_ref, left_ref, up_ref, down_ref,
    neighbours, features, cotangent, active, send_ref, sems,
):
    pairs = (
        (neighbours_any, neighbours), (features_any, features), (cotangent_any, cotangent),
        (active_any, active),
    )
    copies = [pltpu.make_async_copy(s, d, sems.at[t]) for t, (s, d) in enumerate(pairs)]
    for copy in copies:
        copy.start()
    for copy in copies:
        copy.wait()
    choose_sends(neighbours, send_ref)
    for b in range(4):
        mask = active[b : b + 1, :].astype(F32)
        f = features[b].astype(F32)
        values_ref[b * 64 : b * 64 + 64, :] = (mask * (f / (1.0 + jnp.exp(-f)))).astype(BF)
        values_ref[256 + b * 64 : 320 + b * 64, :] = (mask * cotangent[b].astype(F32)).astype(BF)
    faces = dot(values_ref[...], face_matrix()).astype(BF)
    for a in range(2):
        for b in range(4):
            for f in range(6):
                row = (a * 4 + b) * 64
                faces_ref[a, b * 6 + f] = faces[row : row + 64, f * 128 : f * 128 + 128]
    low = low_half((64, 128))
    pack(
        send_ref,
        lambda ids: [jnp.where(low, faces_ref[0, i], faces_ref[1, i]) for i in ids],
        right_ref, left_ref, up_ref, down_ref,
    )


def as_column(row):
    here = lax.broadcasted_iota(jnp.int32, (64, 64), 0)
    there = lax.broadcasted_iota(jnp.int32, (64, 64), 1)
    picked = jnp.where(here == there, jnp.broadcast_to(row, (64, 64)), 0.0)
    return jnp.broadcast_to(jnp.sum(picked, axis=1, keepdims=True), (64, 128))


def prepare_kernel(
    active, first, second, scale, shift,
    mask_ref, w_first, w_back, gain_ref, shift_ref, e_int, e_yz, e_x, windows,
):
    mask_ref[...] = active[...].astype(F32)
    e_int[...], e_yz[...], e_x[...] = spread_matrix(), yz_matrix(), x_matrix()
    windows[...] = window_matrix()
    gain_ref[...] = 1.0 + as_column(scale[...])
    shift_ref[...] = as_column(shift[...])
    for i in range(3):
        for jl in range(9):
            k = 9 * i + jl
            rows, lanes = slice(i * 64, i * 64 + 64), slice(jl * 64, jl * 64 + 64)
            w_first[rows, lanes] = first[k]
            w_back[rows, lanes] = second[26 - k].T


def fill_table(table, faces, arrays, groups):
    low = low_half((64, 128))
    for a in range(arrays):
        for f in range(24):
            table[a, f] = faces[a, f] if arrays == 2 else faces[f]
        table[a, ZERO_ROW] = jnp.zeros((64, 128), BF)
    for ref, base, count in groups:
        for t in range(count * arrays // 2):
            tile = ref[t]
            swapped = jnp.concatenate([tile[:, 64:], tile[:, :64]], axis=1)
            first, second = jnp.where(low, tile, swapped), jnp.where(low, swapped, tile)
            if arrays == 2:
                table[0, base + t], table[1, base + t] = first, second
            else:
                table[0, base + 2 * t], table[0, base + 2 * t + 1] = first, second


def build_padded(index_ref, table, values, ext, side_yz, side_x, e_int, e_yz, e_x, arrays):
    low = low_half((64, 128))
    for a in range(arrays):
        for b in range(4):
            row = (a * 4 + b) * 64
            for side, pairs in ((side_yz, YZ_GROUPS), (side_x, X_GROUPS)):
                for g, (first, second) in enumerate(pairs):
                    lo = index_ref[b * 26 + DIRECTIONS.index(first)]
                    hi = index_ref[b * 26 + DIRECTIONS.index(second)]
                    side[row : row + 64, g * 128 : g * 128 + 128] = jnp.where(
                        low, table[a, lo], table[a, hi]
                    )
    outer = dot(side_x[...], e_x[...]).astype(BF)
    ext[:, 0:128] = outer[:, 0:128]
    ext[:, 1152:1280] = outer[:, 128:256]
    for m in range(4):
        inner = dot(values[:, m * 128 : m * 128 + 128], e_int[...])
        inner = inner + dot(side_yz[...], e_yz[:, m * 256 : m * 256 + 256])
        ext[:, 128 + m * 256 : 384 + m * 256] = inner.astype(BF)


def columns(ext, windows, cols):
    for m in range(5):
        moved = dot(ext[:, m * 256 : m * 256 + 256], windows[...]).astype(BF)
        for a, col in enumerate(cols):
            for b in range(4):
                row = (a * 4 + b) * 64
                lane = b * 640 + m * 128
                for k in range(9):
                    col[k * 64 : k * 64 + 64, lane : lane + 128] = moved[
                        row : row + 64, k * 128 : k * 128 + 128
                    ]


def three_planes(product, lane):
    return (
        product[0:64, lane : lane + 512]
        + product[64:128, lane + 64 : lane + 576]
        + product[128:192, lane + 128 : lane + 640]
    )


def stack_planes(stack, lane, values):
    none = jnp.zeros((64, 64), BF)
    wide = jnp.zeros((64, 128), BF)
    stack[0:64, lane : lane + 640] = jnp.concatenate([values, wide], axis=1)
    stack[64:128, lane : lane + 640] = jnp.concatenate([none, values, none], axis=1)
    stack[128:192, lane : lane + 640] = jnp.concatenate([wide, values], axis=1)


def second_kernel(
    index_ref, values, faces, from_left, from_right, from_up, from_down, mask_ref,
    w_first, w_back, gain_ref, shift_ref, e_int, e_yz, e_x, windows,
    hidden_ref, sums_ref,
    table, ext, side_yz, side_x, col_a, col_s, stack_h, stack_s,
):
    groups = ((from_left, 24, 4), (from_right, 28, 4), (from_up, 32, 6), (from_down, 38, 6))
    fill_table(table, faces, 2, groups)
    build_padded(index_ref, table, values, ext, side_yz, side_x, e_int, e_yz, e_x, 2)
    columns(ext, windows, (col_a, col_s))
    gain = gain_ref[:, 0:1]
    shift = shift_ref[:, 0:1]
    for pair in range(2):
        these = slice(pair * 1280, pair * 1280 + 1280)
        first = dot(w_first[...], col_a[:, these])
        second = dot(w_back[...], col_s[:, these])
        for half in range(2):
            b = 2 * pair + half
            pre, back = three_planes(first, half * 640), three_planes(second, half * 640)
            mask = mask_ref[b : b + 1, :]
            shaped = pre * gain + shift
            gate = 1.0 / (1.0 + jnp.exp(-shaped))
            hidden = (mask * (shaped * gate)).astype(BF)
            slope = (back * mask * gate * (1.0 + shaped * (1.0 - gate)) * gain).astype(BF)
            hidden_ref[b * 64 : b * 64 + 64, :] = hidden
            stack_planes(stack_h, b * 640, hidden)
            stack_planes(stack_s, b * 640, slope)
    total_h = dot_nt(col_s[...], stack_h[...])
    total_s = dot_nt(col_a[...], stack_s[...])
    pack_sums(total_h, total_s, sums_ref)


def faces_kernel(
    send_ref, hidden,
    hidden_faces, right_ref, left_ref, up_ref, down_ref,
):
    out = dot(hidden[...], face_matrix()).astype(BF)
    for b in range(4):
        for f in range(6):
            hidden_faces[b * 6 + f] = out[b * 64 : b * 64 + 64, f * 128 : f * 128 + 128]
    low = low_half((64, 128))
    pack(
        send_ref,
        lambda ids: [
            jnp.where(low, hidden_faces[i], hidden_faces[j]) for i, j in zip(ids[::2], ids[1::2])
        ],
        right_ref, left_ref, up_ref, down_ref,
    )


def pack_sums(total_h, total_s, sums_ref):
    for t, total in enumerate((total_h, total_s)):
        base = t * 864
        sums_ref[base : base + 576, :] = total[:, 0:128].astype(BF)
        sums_ref[base + 576 : base + 864, :] = jnp.concatenate(
            [total[0:288, 128:192], total[288:576, 128:192]], axis=1
        ).astype(BF)
    sums_ref[1728:2048, :] = jnp.zeros((320, 128), BF)


def third_kernel(
    index_ref, hidden_faces, from_left, from_right, from_up, from_down, hidden,
    active, features, weight,
    out_ref,
    table, ext, side_yz, side_x, col, w_second, e_int, e_yz, e_x, windows,
):
    e_int[...], e_yz[...], e_x[...] = spread_matrix(), yz_matrix(), x_matrix()
    windows[...] = window_matrix()
    for i in range(3):
        for jl in range(9):
            w_second[i * 64 : i * 64 + 64, jl * 64 : jl * 64 + 64] = weight[9 * i + jl]
    groups = ((from_left, 24, 4), (from_right, 28, 4), (from_up, 32, 6), (from_down, 38, 6))
    fill_table(table, hidden_faces, 1, groups)
    build_padded(index_ref, table, hidden, ext, side_yz, side_x, e_int, e_yz, e_x, 1)
    columns(ext, windows, (col,))
    for pair in range(2):
        product = dot(w_second[...], col[:, pair * 1280 : pair * 1280 + 1280])
        for half in range(2):
            b = 2 * pair + half
            second = active[b : b + 1, :].astype(F32) * three_planes(product, half * 640)
            out_ref[b] = (features[b].astype(F32) + second).astype(BF)


def share_kernel(parts, left_any, right_any, out_ref):
    total = parts[0].astype(F32)
    for d in range(1, 128):
        total = total + parts[d].astype(F32)
    total = total.astype(BF)
    for d in range(128):
        out_ref[d] = total


def unpack_kernel(sums, first_ref, second_ref):
    for t in range(2):
        base = t * 864
        for i in range(3):
            for jl in range(9):
                if i < 2:
                    block = sums[base + jl * 64 : base + jl * 64 + 64, i * 64 : i * 64 + 64]
                else:
                    pieces = []
                    for r in (jl * 64, jl * 64 + 32):
                        lane, at = (0, r) if r < 288 else (64, r - 288)
                        at += base + 576
                        pieces.append(sums[at : at + 32, lane : lane + 64])
                    block = jnp.concatenate(pieces, axis=0)
                block = block.astype(F32)
                k = 9 * i + jl
                if t == 0:
                    second_ref[26 - k] = block
                else:
                    first_ref[k] = block.T


def sent(array, step):
    pairs = []
    for i in range(32):
        j = i + step
        if 0 <= j < 32 and (abs(step) == GRID_X or i // GRID_X == j // GRID_X):
            pairs.append((i, j))
    return lax.ppermute(array, "brick", pairs)


def forward_kernel(from_left, from_right, up, down, after_any, up_ref, down_ref):
    n = up.shape[0]
    up_ref[0:n] = up[...]
    down_ref[0:n] = down[...]
    for t, ref in enumerate((from_left, from_right)):
        up_ref[n + t * n : 2 * n + t * n] = ref[3 * n :]
        down_ref[n + t * n : 2 * n + t * n] = ref[2 * n : 3 * n]


def first_round(right, left):
    return sent(right, 1), sent(left, -1)


def second_round(from_left, from_right, up, down, after):
    upward, downward = call(
        forward_kernel,
        [(VMEM, t) for t in (from_left, from_right, up, down)] + [(ANY, after)],
        [(VMEM, shape((3 * up.shape[0], 64, 128)))] * 2,
        [],
        8,
        0,
    )
    return from_left, from_right, sent(upward, GRID_X), sent(downward, -GRID_X)


def shape(dims, dtype=BF):
    return jax.ShapeDtypeStruct(dims, dtype)


SMEM = pl.BlockSpec(memory_space=pltpu.SMEM)
VMEM = pl.BlockSpec(memory_space=pltpu.VMEM)
ANY = pl.BlockSpec(memory_space=pl.ANY)
HBM = pl.BlockSpec(memory_space=pltpu.HBM)


def call(kernel, operands, outs, scratch, limit, us):
    return pl.pallas_call(
        kernel,
        out_shape=tuple(o for _, o in outs),
        in_specs=[s for s, _ in operands],
        out_specs=tuple(s for s, _ in outs),
        scratch_shapes=scratch,
        compiler_params=pltpu.CompilerParams(vmem_limit_bytes=limit << 20),
        cost_estimate=pl.CostEstimate(flops=us * 10**9, bytes_accessed=0, transcendentals=0),
        name=kernel.__name__,
    )(*(o for _, o in operands))


def shards(
    features, active, neighbours, first_weight, second_weight, film_scale, film_shift, cotangent
):
    def messages(arrays):
        return [(VMEM, shape((n * arrays, 64, 128))) for n in (4, 4, 1, 1)]


    values, faces, *outgoing = call(
        first_kernel,
        [(HBM, t) for t in (neighbours, features, cotangent, active)],
        [(VMEM, shape((512, 512))), (VMEM, shape((2, 24, 64, 128)))]
        + messages(2),
        [
            pltpu.SMEM((4, 26), jnp.int32),
            pltpu.VMEM((4, 64, 512), BF),
            pltpu.VMEM((4, 64, 512), BF),
            pltpu.VMEM((4, 512), jnp.int32),
            pltpu.SMEM((80,), jnp.int32),
            pltpu.SemaphoreType.DMA((4,)),
        ],
        58,
        4,
    )
    arrived = second_round(*first_round(*outgoing[:2]), *outgoing[2:], neighbours)
    index, send_ids = call(
        tables_kernel,
        [(HBM, neighbours), (ANY, arrived[0])],
        [(SMEM, shape((104,), jnp.int32)), (SMEM, shape((80,), jnp.int32))],
        [
            pltpu.SMEM((4, 26), jnp.int32),
            pltpu.SMEM((10,), jnp.int32),
            pltpu.SMEM((104,), jnp.int32),
            pltpu.SMEM((240,), jnp.int32),
            pltpu.SemaphoreType.DMA,
        ],
        8,
        3,
    )
    spread_shapes = [(128, 256), (512, 1024), (1152, 256), (256, 1152)]
    prepared = call(
        prepare_kernel,
        [
            (VMEM, t)
            for t in (
                active,
                first_weight,
                second_weight,
                film_scale.reshape(1, 64),
                film_shift.reshape(1, 64),
            )
        ],
        [(VMEM, shape((4, 512), F32))]
        + [(VMEM, shape((192, 576)))] * 2
        + [(VMEM, shape((64, 128), F32))] * 2
        + [(VMEM, shape(dims)) for dims in spread_shapes],
        [],
        16,
        3,
    )
    mask, w_first, w_back, gain, shift, *spreads = prepared

    hidden, sums = call(
        second_kernel,
        [(SMEM, index)]
        + [(VMEM, t) for t in (values, faces, *arrived, mask, w_first, w_back, gain, shift)]
        + [(VMEM, t) for t in spreads],
        [
            (VMEM, shape((256, 512))),
            (VMEM, shape((2048, 128))),
        ],
        [
            pltpu.VMEM((2, 45, 64, 128), BF),
            pltpu.VMEM((512, 1280), BF),
            pltpu.VMEM((512, 512), BF),
            pltpu.VMEM((512, 1152), BF),
            pltpu.VMEM((576, 2560), BF),
            pltpu.VMEM((576, 2560), BF),
            pltpu.VMEM((192, 2560), BF),
            pltpu.VMEM((192, 2560), BF),
        ],
        32,
        10,
    )
    parts = lax.all_to_all(sums.reshape(128, 16, 128), AXES, 0, 0, tiled=True)
    hidden_faces, *outgoing = call(
        faces_kernel,
        [(SMEM, send_ids), (VMEM, hidden)],
        [(VMEM, shape((24, 64, 128)))] + messages(1),
        [],
        16,
        8,
    )
    sides = first_round(*outgoing[:2])
    (shares,) = call(
        share_kernel, [(VMEM, parts)] + [(ANY, t) for t in sides], [(VMEM, shape((128, 16, 128)))], [], 16, 1
    )
    arrived = second_round(*sides, *outgoing[2:], shares)
    sums = lax.all_to_all(shares, AXES, 0, 0, tiled=True)
    (block_output,) = call(
        third_kernel,
        [(SMEM, index)]
        + [(VMEM, t) for t in (hidden_faces, *arrived, hidden, active, features, second_weight)],
        [(VMEM, shape((4, 64, 512)))],
        [
            pltpu.VMEM((1, 45, 64, 128), BF),
            pltpu.VMEM((256, 1280), BF),
            pltpu.VMEM((256, 512), BF),
            pltpu.VMEM((256, 1152), BF),
            pltpu.VMEM((576, 2560), BF),
            pltpu.VMEM((192, 576), BF),
        ]
        + [pltpu.VMEM(dims, BF) for dims in spread_shapes],
        16,
        2,
    )
    grad_first, grad_second = call(
        unpack_kernel,
        [(VMEM, sums.reshape(2048, 128))],
        [(VMEM, shape((27, 64, 64), F32))] * 2,
        [],
        16,
        0,
    )
    return block_output, grad_first, grad_second


def solution(mesh):
    split = P(AXES, None, None)
    rows = P(AXES, None)
    return jax.shard_map(
        shards,
        mesh=mesh,
        in_specs=(split, rows, rows, P(), P(), P(), P(), split),
        out_specs=(split, P(), P()),
        check_vma=False,
    )
```

```python
import jax
import jax.numpy as jnp
from jax import lax
from jax.experimental import pallas as pl
from jax.experimental.pallas import tpu as pltpu
from jax.sharding import PartitionSpec as P

AXES = ("region", "brick")
GRID_X = 8
ZERO_ROW = 44
ARRIVALS = {
    (-1, 0): (24, 4),
    (1, 0): (28, 4),
    (0, -1): (32, 2),
    (-1, -1): (34, 2),
    (1, -1): (36, 2),
    (0, 1): (38, 2),
    (-1, 1): (40, 2),
    (1, 1): (42, 2),
}
BF = jnp.bfloat16
F32 = jnp.float32


def direction_list():
    return [
        (a, b, c)
        for a in (-1, 0, 1)
        for b in (-1, 0, 1)
        for c in (-1, 0, 1)
        if (a, b, c) != (0, 0, 0)
    ]


DIRECTIONS = direction_list()


def face_of(vector):
    if vector[0] != 0:
        return 0 if vector[0] < 0 else 1
    if vector[1] != 0:
        return 2 if vector[1] < 0 else 3
    return 4 if vector[2] < 0 else 5


SEND_FACE = [face_of(d) for d in DIRECTIONS]
READ_FACE = [face_of(tuple(-t for t in d)) for d in DIRECTIONS]


X_TILES = [(0, 0), (0, None), (None, 0), (None, None)]
Y_TILES = [(0, 0), (0, None)]


def one_hot(rows, source):
    at = lax.broadcasted_iota(jnp.int32, (rows, source.shape[1]), 0)
    return jnp.where(at == source, 1.0, 0.0).astype(BF)


def lanes(count):
    return lax.broadcasted_iota(jnp.int32, (1, count), 1)


def face_matrix():
    lane = lanes(768)
    face, u, v = lane >> 7, (lane >> 3) & 7, lane & 7
    first = jnp.where(face < 2, u * 8 + v, jnp.where(face < 4, u * 64 + v, u * 64 + v * 8))
    far = jnp.where(face == 1, 448, jnp.where(face == 3, 56, jnp.where(face == 5, 7, 0)))
    return one_hot(512, first + far)


def padded_lane(count):
    lane = lanes(count)
    cell = lane & 127
    y = (cell * 205) >> 11
    return lane >> 7, y, cell - y * 10


def window_matrix():
    lane = lanes(1152)
    tap, plane, y, z = lane >> 7, (lane >> 6) & 1, (lane >> 3) & 7, lane & 7
    j = jnp.where(tap < 3, 0, jnp.where(tap < 6, 1, 2))
    return one_hot(256, plane * 128 + (y + j) * 10 + z + tap - 3 * j)


def yz_matrix():
    x, y, z = padded_lane(1024)
    y_edge, z_edge = (y == 0) | (y == 9), (z == 0) | (z == 9)
    z_cell = jnp.where(z == 0, 7, jnp.where(z == 9, 0, z - 1))
    from_y = jnp.where(z_edge, 128, 0) + jnp.where(y == 0, 64, 0) + x * 8 + z_cell
    from_z = 256 + jnp.where(z == 0, 64, 0) + x * 8 + y - 1
    own = 384 + (x & 1) * 64 + (y - 1) * 8 + z - 1
    source = jnp.where(y_edge, from_y, jnp.where(z_edge, from_z, own))
    return one_hot(512, jnp.where(y < 10, source, -1))


def x_matrix():
    side, y, z = padded_lane(256)
    y_edge, z_edge = (y == 0) | (y == 9), (z == 0) | (z == 9)
    y_cell = jnp.where(y == 0, 7, jnp.where(y == 9, 0, y - 1))
    z_cell = jnp.where(z == 0, 7, jnp.where(z == 9, 0, z - 1))
    tile = jnp.where(y_edge, 256, 0) + jnp.where(z_edge, 128, 0)
    source = tile + jnp.where(side == 0, 64, 0) + y_cell * 8 + z_cell
    return one_hot(512, jnp.where(y < 10, source, -1))


def dot(a, b):
    return lax.dot_general(a, b, (((1,), (0,)), ((), ())), preferred_element_type=F32)


def dot_nt(a, b):
    return lax.dot_general(a, b, (((1,), (1,)), ((), ())), preferred_element_type=F32)


def low_half(shape):
    return lax.broadcasted_iota(jnp.int32, shape, len(shape) - 1) < 64


def place(n, origin):
    return jnp.where(n >= 0, ((n >> 5) & 3) * 3 + ((n >> 2) & 7) + origin, 9)


def own_origin():
    mine = lax.axis_index("brick")
    return 4 - (mine >> 3) * 3 - (mine & 7)


def choose_sends(neighbours, send_ref, seen=None):
    origin = own_origin()
    readers = []
    for b in range(4):
        bits = [0] * 6
        for e in range(26):
            n = neighbours[b, e]
            where = place(n, origin)
            bits[SEND_FACE[e]] = bits[SEND_FACE[e]] | jnp.left_shift(1, where)
            if seen is not None:
                seen(b, e, n, where)
        readers += bits
    for x, y in ARRIVALS:
        s = (y + 1) * 3 + x + 1
        for t in range(4):
            send_ref[s * 32 + t] = 0
        sent = s * 32
        for f in range(24):
            send_ref[sent] = f
            sent = sent + ((readers[f] >> s) & 1)


def tables_kernel(
    neighbours_any, after_any, index_ref, send_ref, neighbours, held, rank_ref, sem
):
    copy = pltpu.make_async_copy(neighbours_any, neighbours, sem)
    copy.start()
    for s in range(10):
        held[s] = 0
    for f in range(24):
        rank_ref[4 * 24 + f] = f
        rank_ref[9 * 24 + f] = ZERO_ROW
    rows = {}

    def mark(b, e, n, where):
        face = (n & 3) * 6 + READ_FACE[e]
        rows[b, e] = where * 24 + face
        held[where] = held[where] | jnp.left_shift(1, face)

    copy.wait()
    choose_sends(neighbours, send_ref, mark)
    for (x, y), (base, count) in ARRIVALS.items():
        s = (y + 1) * 3 + x + 1
        bits = held[s]
        got = base
        for f in range(24):
            rank_ref[s * 24 + f] = jnp.minimum(got, base + count - 1)
            got = got + ((bits >> f) & 1)
    for (b, e), row in rows.items():
        index_ref[b * 26 + e] = rank_ref[row]


def send_slots(send_ref, x, y):
    s = (y + 1) * 3 + x + 1
    return [send_ref[s * 32 + t] for t in range(4 if y == 0 else 2)]


def pack(send_ref, tiles_of, right_ref, left_ref, up_ref, down_ref):
    for ref, x in ((right_ref, 1), (left_ref, -1)):
        ids = send_slots(send_ref, x, 0) + send_slots(send_ref, x, -1) + send_slots(send_ref, x, 1)
        for t, tile in enumerate(tiles_of(ids)):
            ref[t] = tile
    for ref, y in ((up_ref, 1), (down_ref, -1)):
        for t, tile in enumerate(tiles_of(send_slots(send_ref, 0, y))):
            ref[t] = tile


def first_kernel(
    neighbours_any, features_any, cotangent_any, active_any,
    values_ref, faces_ref, right_ref, left_ref, up_ref, down_ref,
    neighbours, features, cotangent, active, send_ref, sems,
):
    pairs = (
        (neighbours_any, neighbours), (features_any, features), (cotangent_any, cotangent),
        (active_any, active),
    )
    copies = [pltpu.make_async_copy(s, d, sems.at[t]) for t, (s, d) in enumerate(pairs)]
    for copy in copies:
        copy.start()
    for copy in copies:
        copy.wait()
    choose_sends(neighbours, send_ref)
    for b in range(4):
        mask = active[b : b + 1, :].astype(F32)
        f = features[b].astype(F32)
        values_ref[b * 64 : b * 64 + 64, :] = (mask * (f / (1.0 + jnp.exp(-f)))).astype(BF)
        values_ref[256 + b * 64 : 320 + b * 64, :] = (mask * cotangent[b].astype(F32)).astype(BF)
    faces = dot(values_ref[...], face_matrix()).astype(BF)
    for a in range(2):
        for b in range(4):
            for f in range(6):
                row = (a * 4 + b) * 64
                faces_ref[a, b * 6 + f] = faces[row : row + 64, f * 128 : f * 128 + 128]
    low = low_half((64, 128))
    pack(
        send_ref,
        lambda ids: [jnp.where(low, faces_ref[0, i], faces_ref[1, i]) for i in ids],
        right_ref, left_ref, up_ref, down_ref,
    )


def as_column(row):
    here = lax.broadcasted_iota(jnp.int32, (64, 64), 0)
    there = lax.broadcasted_iota(jnp.int32, (64, 64), 1)
    picked = jnp.where(here == there, jnp.broadcast_to(row, (64, 64)), 0.0)
    return jnp.broadcast_to(jnp.sum(picked, axis=1, keepdims=True), (64, 128))


def prepare_kernel(
    active, first, second, scale, shift,
    mask_ref, w_first, w_back, gain_ref, shift_ref, e_yz, e_x, windows,
):
    mask_ref[...] = active[...].astype(F32)
    e_yz[...], e_x[...], windows[...] = yz_matrix(), x_matrix(), window_matrix()
    gain_ref[...] = 1.0 + as_column(scale[...])
    shift_ref[...] = as_column(shift[...])
    for i in range(3):
        for jl in range(9):
            k = 9 * i + jl
            rows, lanes = slice(i * 64, i * 64 + 64), slice(jl * 64, jl * 64 + 64)
            w_first[rows, lanes] = first[k]
            w_back[rows, lanes] = second[26 - k].T


def fill_table(table, faces, arrays, groups):
    low = low_half((64, 128))
    for a in range(arrays):
        for f in range(24):
            table[a, f] = faces[a, f] if arrays == 2 else faces[f]
        table[a, ZERO_ROW] = jnp.zeros((64, 128), BF)
    for ref, base, count in groups:
        for t in range(count * arrays // 2):
            tile = ref[t]
            swapped = jnp.concatenate([tile[:, 64:], tile[:, :64]], axis=1)
            first, second = jnp.where(low, tile, swapped), jnp.where(low, swapped, tile)
            if arrays == 2:
                table[0, base + t], table[1, base + t] = first, second
            else:
                table[0, base + 2 * t], table[0, base + 2 * t + 1] = first, second


def build_padded(index_ref, table, values, ext, side_yz, side_x, e_yz, e_x, arrays):
    lane = lax.broadcasted_iota(jnp.int32, (64, 128), 1)
    low, u_far, v_far = lane < 64, (lane & 32) != 0, (lane & 4) != 0
    for a in range(arrays):
        for b in range(4):
            row = (a * 4 + b) * 64

            def face(*offset):
                return table[a, index_ref[b * 26 + DIRECTIONS.index(offset)]]

            def both(low_face, high_face):
                return jnp.where(low, low_face, high_face)

            def along_v(u, v, make):
                if v is None:
                    return jnp.where(v_far, make(u, -1), make(u, 1))
                return make(u, v)

            def tile(u, v, make):
                if u is None:
                    return jnp.where(u_far, along_v(-1, v, make), along_v(1, v, make))
                return along_v(u, v, make)

            def x_faces(y, z):
                return both(face(1, y, z), face(-1, y, z))

            for t, (y, z) in enumerate(X_TILES):
                side_x[row : row + 64, t * 128 : t * 128 + 128] = tile(y, z, x_faces)

            def y_faces(_, z):
                return both(face(0, 1, z), face(0, -1, z))

            for t, (_, z) in enumerate(Y_TILES):
                side_yz[row : row + 64, t * 128 : t * 128 + 128] = along_v(0, z, y_faces)
            side_yz[row : row + 64, 256:384] = both(face(0, 0, 1), face(0, 0, -1))
    outer = dot(side_x[...], e_x[...]).astype(BF)
    ext[:, 0:128] = outer[:, 0:128]
    ext[:, 1152:1280] = outer[:, 128:256]
    for m in range(4):
        known = jnp.concatenate([side_yz[...], values[:, m * 128 : m * 128 + 128]], axis=1)
        inner = dot(known, e_yz[:, m * 256 : m * 256 + 256])
        ext[:, 128 + m * 256 : 384 + m * 256] = inner.astype(BF)


def columns(ext, windows, cols):
    for m in range(5):
        moved = dot(ext[:, m * 256 : m * 256 + 256], windows[...]).astype(BF)
        for a, col in enumerate(cols):
            for b in range(4):
                row = (a * 4 + b) * 64
                lane = b * 640 + m * 128
                for k in range(9):
                    col[k * 64 : k * 64 + 64, lane : lane + 128] = moved[
                        row : row + 64, k * 128 : k * 128 + 128
                    ]


def three_planes(product, lane):
    return (
        product[0:64, lane : lane + 512]
        + product[64:128, lane + 64 : lane + 576]
        + product[128:192, lane + 128 : lane + 640]
    )


def stack_planes(stack, lane, values):
    none = jnp.zeros((64, 64), BF)
    wide = jnp.zeros((64, 128), BF)
    stack[0:64, lane : lane + 640] = jnp.concatenate([values, wide], axis=1)
    stack[64:128, lane : lane + 640] = jnp.concatenate([none, values, none], axis=1)
    stack[128:192, lane : lane + 640] = jnp.concatenate([wide, values], axis=1)


def second_kernel(
    index_ref, values, faces, from_left, from_right, from_up, from_down, mask_ref,
    w_first, w_back, gain_ref, shift_ref, e_yz, e_x, windows,
    hidden_ref, sums_ref,
    table, ext, side_yz, side_x, col_a, col_s, stack_h, stack_s,
):
    groups = ((from_left, 24, 4), (from_right, 28, 4), (from_up, 32, 6), (from_down, 38, 6))
    fill_table(table, faces, 2, groups)
    build_padded(index_ref, table, values, ext, side_yz, side_x, e_yz, e_x, 2)
    columns(ext, windows, (col_a, col_s))
    gain = gain_ref[:, 0:1]
    shift = shift_ref[:, 0:1]
    for pair in range(2):
        these = slice(pair * 1280, pair * 1280 + 1280)
        first = dot(w_first[...], col_a[:, these])
        second = dot(w_back[...], col_s[:, these])
        for half in range(2):
            b = 2 * pair + half
            pre, back = three_planes(first, half * 640), three_planes(second, half * 640)
            mask = mask_ref[b : b + 1, :]
            shaped = pre * gain + shift
            gate = 1.0 / (1.0 + jnp.exp(-shaped))
            hidden = (mask * (shaped * gate)).astype(BF)
            slope = (back * mask * gate * (1.0 + shaped * (1.0 - gate)) * gain).astype(BF)
            hidden_ref[b * 64 : b * 64 + 64, :] = hidden
            stack_planes(stack_h, b * 640, hidden)
            stack_planes(stack_s, b * 640, slope)
    total_h = dot_nt(col_s[...], stack_h[...])
    total_s = dot_nt(col_a[...], stack_s[...])
    pack_sums(total_h, total_s, sums_ref)


def faces_kernel(
    send_ref, hidden,
    hidden_faces, right_ref, left_ref, up_ref, down_ref,
):
    out = dot(hidden[...], face_matrix()).astype(BF)
    for b in range(4):
        for f in range(6):
            hidden_faces[b * 6 + f] = out[b * 64 : b * 64 + 64, f * 128 : f * 128 + 128]
    low = low_half((64, 128))
    pack(
        send_ref,
        lambda ids: [
            jnp.where(low, hidden_faces[i], hidden_faces[j]) for i, j in zip(ids[::2], ids[1::2])
        ],
        right_ref, left_ref, up_ref, down_ref,
    )


def pack_sums(total_h, total_s, sums_ref):
    for t, total in enumerate((total_h, total_s)):
        base = t * 864
        sums_ref[base : base + 576, :] = total[:, 0:128].astype(BF)
        sums_ref[base + 576 : base + 864, :] = jnp.concatenate(
            [total[0:288, 128:192], total[288:576, 128:192]], axis=1
        ).astype(BF)
    sums_ref[1728:2048, :] = jnp.zeros((320, 128), BF)


def third_kernel(
    index_ref, hidden_faces, from_left, from_right, from_up, from_down, hidden,
    active, features, weight,
    out_ref,
    table, ext, side_yz, side_x, col, w_second, e_yz, e_x, windows,
):
    e_yz[...], e_x[...], windows[...] = yz_matrix(), x_matrix(), window_matrix()
    for i in range(3):
        for jl in range(9):
            w_second[i * 64 : i * 64 + 64, jl * 64 : jl * 64 + 64] = weight[9 * i + jl]
    groups = ((from_left, 24, 4), (from_right, 28, 4), (from_up, 32, 6), (from_down, 38, 6))
    fill_table(table, hidden_faces, 1, groups)
    build_padded(index_ref, table, hidden, ext, side_yz, side_x, e_yz, e_x, 1)
    columns(ext, windows, (col,))
    for pair in range(2):
        product = dot(w_second[...], col[:, pair * 1280 : pair * 1280 + 1280])
        for half in range(2):
            b = 2 * pair + half
            second = active[b : b + 1, :].astype(F32) * three_planes(product, half * 640)
            out_ref[b] = (features[b].astype(F32) + second).astype(BF)


def share_kernel(parts, left_any, right_any, out_ref):
    totals = [parts[d].astype(F32) for d in range(4)]
    for d in range(4, 128):
        totals[d % 4] = totals[d % 4] + parts[d].astype(F32)
    total = ((totals[0] + totals[1]) + (totals[2] + totals[3])).astype(BF)
    for d in range(128):
        out_ref[d] = total


def unpack_kernel(sums, first_any, second_any, first, second, sems):
    copies = []
    for t, (grad, grad_any) in enumerate(((second, second_any), (first, first_any))):
        base = t * 864
        for i in range(3):
            for jl in range(9):
                if i < 2:
                    block = sums[base + jl * 64 : base + jl * 64 + 64, i * 64 : i * 64 + 64]
                else:
                    pieces = []
                    for r in (jl * 64, jl * 64 + 32):
                        lane, at = (0, r) if r < 288 else (64, r - 288)
                        at += base + 576
                        pieces.append(sums[at : at + 32, lane : lane + 64])
                    block = jnp.concatenate(pieces, axis=0)
                block = block.astype(F32)
                k = 9 * i + jl
                if t == 0:
                    grad[26 - k] = block
                else:
                    grad[k] = block.T
            nine = pl.ds(18 - 9 * i if t == 0 else 9 * i, 9)
            copies.append(
                pltpu.make_async_copy(grad.at[nine], grad_any.at[nine], sems.at[3 * t + i])
            )
            copies[-1].start()
    for copy in copies:
        copy.wait()


def sent(array, step):
    pairs = []
    for i in range(32):
        j = i + step
        if 0 <= j < 32 and (abs(step) == GRID_X or i // GRID_X == j // GRID_X):
            pairs.append((i, j))
    return lax.ppermute(array, "brick", pairs)


def forward_kernel(from_left, from_right, up, down, after_any, up_ref, down_ref):
    n = up.shape[0]
    up_ref[0:n] = up[...]
    down_ref[0:n] = down[...]
    for t, ref in enumerate((from_left, from_right)):
        up_ref[n + t * n : 2 * n + t * n] = ref[3 * n :]
        down_ref[n + t * n : 2 * n + t * n] = ref[2 * n : 3 * n]


def first_round(right, left):
    return sent(right, 1), sent(left, -1)


def second_round(from_left, from_right, up, down, after):
    upward, downward = call(
        forward_kernel,
        [(VMEM, t) for t in (from_left, from_right, up, down)] + [(ANY, after)],
        [(VMEM, shape((3 * up.shape[0], 64, 128)))] * 2,
        [],
        8,
        0,
    )
    return from_left, from_right, sent(upward, GRID_X), sent(downward, -GRID_X)


def shape(dims, dtype=BF):
    return jax.ShapeDtypeStruct(dims, dtype)


SMEM = pl.BlockSpec(memory_space=pltpu.SMEM)
VMEM = pl.BlockSpec(memory_space=pltpu.VMEM)
ANY = pl.BlockSpec(memory_space=pl.ANY)
HBM = pl.BlockSpec(memory_space=pltpu.HBM)


def call(kernel, operands, outs, scratch, limit, us):
    return pl.pallas_call(
        kernel,
        out_shape=tuple(o for _, o in outs),
        in_specs=[s for s, _ in operands],
        out_specs=tuple(s for s, _ in outs),
        scratch_shapes=scratch,
        compiler_params=pltpu.CompilerParams(vmem_limit_bytes=limit << 20),
        cost_estimate=pl.CostEstimate(flops=us * 10**9, bytes_accessed=0, transcendentals=0),
        name=kernel.__name__,
    )(*(o for _, o in operands))


def shards(
    features, active, neighbours, first_weight, second_weight, film_scale, film_shift, cotangent
):
    def messages(arrays):
        return [(VMEM, shape((n * arrays, 64, 128))) for n in (4, 4, 1, 1)]


    values, faces, *outgoing = call(
        first_kernel,
        [(HBM, t) for t in (neighbours, features, cotangent, active)],
        [(VMEM, shape((512, 512))), (VMEM, shape((2, 24, 64, 128)))]
        + messages(2),
        [
            pltpu.SMEM((4, 26), jnp.int32),
            pltpu.VMEM((4, 64, 512), BF),
            pltpu.VMEM((4, 64, 512), BF),
            pltpu.VMEM((4, 512), jnp.int32),
            pltpu.SMEM((288,), jnp.int32),
            pltpu.SemaphoreType.DMA((4,)),
        ],
        58,
        4,
    )
    arrived = second_round(*first_round(*outgoing[:2]), *outgoing[2:], outgoing[2])
    index, send_ids = call(
        tables_kernel,
        [(HBM, neighbours), (ANY, arrived[0])],
        [(SMEM, shape((104,), jnp.int32)), (SMEM, shape((288,), jnp.int32))],
        [
            pltpu.SMEM((4, 26), jnp.int32),
            pltpu.SMEM((10,), jnp.int32),
            pltpu.SMEM((240,), jnp.int32),
            pltpu.SemaphoreType.DMA,
        ],
        8,
        3,
    )
    spread_shapes = [(512, 1024), (512, 256), (256, 1152)]
    prepared = call(
        prepare_kernel,
        [
            (VMEM, t)
            for t in (
                active,
                first_weight,
                second_weight,
                film_scale.reshape(1, 64),
                film_shift.reshape(1, 64),
            )
        ],
        [(VMEM, shape((4, 512), F32))]
        + [(VMEM, shape((192, 576)))] * 2
        + [(VMEM, shape((64, 128), F32))] * 2
        + [(VMEM, shape(dims)) for dims in spread_shapes],
        [],
        16,
        3,
    )
    mask, w_first, w_back, gain, shift, *spreads = prepared

    hidden, sums = call(
        second_kernel,
        [(SMEM, index)]
        + [(VMEM, t) for t in (values, faces, *arrived, mask, w_first, w_back, gain, shift)]
        + [(VMEM, t) for t in spreads],
        [
            (VMEM, shape((256, 512))),
            (VMEM, shape((2048, 128))),
        ],
        [
            pltpu.VMEM((2, 45, 64, 128), BF),
            pltpu.VMEM((512, 1280), BF),
            pltpu.VMEM((512, 384), BF),
            pltpu.VMEM((512, 512), BF),
            pltpu.VMEM((576, 2560), BF),
            pltpu.VMEM((576, 2560), BF),
            pltpu.VMEM((192, 2560), BF),
            pltpu.VMEM((192, 2560), BF),
        ],
        32,
        10,
    )
    parts = lax.all_to_all(sums.reshape(128, 16, 128), AXES, 0, 0, tiled=True)
    hidden_faces, *outgoing = call(
        faces_kernel,
        [(SMEM, send_ids), (VMEM, hidden)],
        [(VMEM, shape((24, 64, 128)))] + messages(1),
        [],
        16,
        8,
    )
    sides = first_round(*outgoing[:2])
    (shares,) = call(
        share_kernel, [(VMEM, parts)] + [(ANY, t) for t in sides], [(VMEM, shape((128, 16, 128)))], [], 16, 1
    )
    arrived = second_round(*sides, *outgoing[2:], shares)
    sums = lax.all_to_all(shares, AXES, 0, 0, tiled=True)
    (block_output,) = call(
        third_kernel,
        [(SMEM, index)]
        + [(VMEM, t) for t in (hidden_faces, *arrived, hidden, active, features, second_weight)],
        [(VMEM, shape((4, 64, 512)))],
        [
            pltpu.VMEM((1, 45, 64, 128), BF),
            pltpu.VMEM((256, 1280), BF),
            pltpu.VMEM((256, 384), BF),
            pltpu.VMEM((256, 512), BF),
            pltpu.VMEM((576, 2560), BF),
            pltpu.VMEM((192, 576), BF),
        ]
        + [pltpu.VMEM(dims, BF) for dims in spread_shapes],
        16,
        2,
    )
    grad_first, grad_second = call(
        unpack_kernel,
        [(VMEM, sums.reshape(2048, 128))],
        [(ANY, shape((27, 64, 64), F32))] * 2,
        [
            pltpu.VMEM((27, 64, 64), F32),
            pltpu.VMEM((27, 64, 64), F32),
            pltpu.SemaphoreType.DMA((6,)),
        ],
        16,
        0,
    )
    return block_output, grad_first, grad_second


def solution(mesh):
    split = P(AXES, None, None)
    rows = P(AXES, None)
    return jax.shard_map(
        shards,
        mesh=mesh,
        in_specs=(split, rows, rows, P(), P(), P(), P(), split),
        out_specs=(split, P(), P()),
        check_vma=False,
    )
```

```python
import jax
import jax.numpy as jnp
from jax import lax
from jax.experimental import pallas as pl
from jax.experimental.pallas import tpu as pltpu
from jax.sharding import PartitionSpec as P

AXES = ("region", "brick")
GRID_X = 8
ZERO_ROW = 44
ARRIVALS = {
    (-1, 0): (24, 4),
    (1, 0): (28, 4),
    (0, -1): (32, 2),
    (-1, -1): (34, 2),
    (1, -1): (36, 2),
    (0, 1): (38, 2),
    (-1, 1): (40, 2),
    (1, 1): (42, 2),
}
BF = jnp.bfloat16
F32 = jnp.float32


def direction_list():
    return [
        (a, b, c)
        for a in (-1, 0, 1)
        for b in (-1, 0, 1)
        for c in (-1, 0, 1)
        if (a, b, c) != (0, 0, 0)
    ]


DIRECTIONS = direction_list()


def face_of(vector):
    if vector[0] != 0:
        return 0 if vector[0] < 0 else 1
    if vector[1] != 0:
        return 2 if vector[1] < 0 else 3
    return 4 if vector[2] < 0 else 5


SEND_FACE = [face_of(d) for d in DIRECTIONS]
READ_FACE = [face_of(tuple(-t for t in d)) for d in DIRECTIONS]


X_TILES = [(0, 0), (0, None), (None, 0), (None, None)]
Y_TILES = [(0, 0), (0, None)]


def one_hot(rows, source):
    at = lax.broadcasted_iota(jnp.int32, (rows, source.shape[1]), 0)
    return jnp.where(at == source, 1.0, 0.0).astype(BF)


def lanes(count):
    return lax.broadcasted_iota(jnp.int32, (1, count), 1)


def face_matrix():
    lane = lanes(768)
    face, u, v = lane >> 7, (lane >> 3) & 7, lane & 7
    first = jnp.where(face < 2, u * 8 + v, jnp.where(face < 4, u * 64 + v, u * 64 + v * 8))
    far = jnp.where(face == 1, 448, jnp.where(face == 3, 56, jnp.where(face == 5, 7, 0)))
    return one_hot(512, first + far)


def padded_lane(count):
    lane = lanes(count)
    cell = lane & 127
    y = (cell * 205) >> 11
    return lane >> 7, y, cell - y * 10


def window_matrix():
    lane = lanes(1152)
    tap, plane, y, z = lane >> 7, (lane >> 6) & 1, (lane >> 3) & 7, lane & 7
    j = jnp.where(tap < 3, 0, jnp.where(tap < 6, 1, 2))
    return one_hot(256, plane * 128 + (y + j) * 10 + z + tap - 3 * j)


def yz_matrix():
    x, y, z = padded_lane(1024)
    y_edge, z_edge = (y == 0) | (y == 9), (z == 0) | (z == 9)
    z_cell = jnp.where(z == 0, 7, jnp.where(z == 9, 0, z - 1))
    from_y = jnp.where(z_edge, 128, 0) + jnp.where(y == 0, 64, 0) + x * 8 + z_cell
    from_z = 256 + jnp.where(z == 0, 64, 0) + x * 8 + y - 1
    own = 384 + (x & 1) * 64 + (y - 1) * 8 + z - 1
    source = jnp.where(y_edge, from_y, jnp.where(z_edge, from_z, own))
    return one_hot(512, jnp.where(y < 10, source, -1))


def x_matrix():
    side, y, z = padded_lane(256)
    y_edge, z_edge = (y == 0) | (y == 9), (z == 0) | (z == 9)
    y_cell = jnp.where(y == 0, 7, jnp.where(y == 9, 0, y - 1))
    z_cell = jnp.where(z == 0, 7, jnp.where(z == 9, 0, z - 1))
    tile = jnp.where(y_edge, 256, 0) + jnp.where(z_edge, 128, 0)
    source = tile + jnp.where(side == 0, 64, 0) + y_cell * 8 + z_cell
    return one_hot(512, jnp.where(y < 10, source, -1))


def dot(a, b):
    return lax.dot_general(a, b, (((1,), (0,)), ((), ())), preferred_element_type=F32)


def dot_nt(a, b):
    return lax.dot_general(a, b, (((1,), (1,)), ((), ())), preferred_element_type=F32)


def low_half(shape):
    return lax.broadcasted_iota(jnp.int32, shape, len(shape) - 1) < 64


def place(n, origin):
    return jnp.where(n >= 0, ((n >> 5) & 3) * 3 + ((n >> 2) & 7) + origin, 9)


def own_origin():
    mine = lax.axis_index("brick")
    return 4 - (mine >> 3) * 3 - (mine & 7)


def choose_sends(neighbours, send_ref, seen=None):
    origin = own_origin()
    readers = []
    for b in range(4):
        bits = [0] * 6
        for e in range(26):
            n = neighbours[b, e]
            where = place(n, origin)
            bits[SEND_FACE[e]] = bits[SEND_FACE[e]] | jnp.left_shift(1, where)
            if seen is not None:
                seen(b, e, n, where)
        readers += bits
    for x, y in ARRIVALS:
        s = (y + 1) * 3 + x + 1
        for t in range(4):
            send_ref[s * 32 + t] = 0
        sent = s * 32
        for f in range(24):
            send_ref[sent] = f
            sent = sent + ((readers[f] >> s) & 1)


def tables_kernel(
    neighbours_any, after_any, index_ref, send_ref, neighbours, held, rank_ref, sem
):
    copy = pltpu.make_async_copy(neighbours_any, neighbours, sem)
    copy.start()
    for s in range(10):
        held[s] = 0
    for f in range(24):
        rank_ref[4 * 24 + f] = f
        rank_ref[9 * 24 + f] = ZERO_ROW
    rows = {}

    def mark(b, e, n, where):
        face = (n & 3) * 6 + READ_FACE[e]
        rows[b, e] = where * 24 + face
        held[where] = held[where] | jnp.left_shift(1, face)

    copy.wait()
    choose_sends(neighbours, send_ref, mark)
    for (x, y), (base, count) in ARRIVALS.items():
        s = (y + 1) * 3 + x + 1
        bits = held[s]
        got = base
        for f in range(24):
            rank_ref[s * 24 + f] = jnp.minimum(got, base + count - 1)
            got = got + ((bits >> f) & 1)
    for (b, e), row in rows.items():
        index_ref[b * 26 + e] = rank_ref[row]


def send_slots(send_ref, x, y):
    s = (y + 1) * 3 + x + 1
    return [send_ref[s * 32 + t] for t in range(4 if y == 0 else 2)]


def pack(send_ref, tiles_of, right_ref, left_ref, up_ref, down_ref):
    for ref, x in ((right_ref, 1), (left_ref, -1)):
        ids = send_slots(send_ref, x, 0) + send_slots(send_ref, x, -1) + send_slots(send_ref, x, 1)
        for t, tile in enumerate(tiles_of(ids)):
            ref[t] = tile
    for ref, y in ((up_ref, 1), (down_ref, -1)):
        for t, tile in enumerate(tiles_of(send_slots(send_ref, 0, y))):
            ref[t] = tile


def own_faces(values, faces_ref):
    faces = dot(values[...], face_matrix()).astype(BF)
    for a in range(2):
        for b in range(4):
            for f in range(6):
                row = (a * 4 + b) * 64
                faces_ref[a, b * 6 + f] = faces[row : row + 64, f * 128 : f * 128 + 128]


def first_kernel(
    neighbours_any, features_any, cotangent_any, active_any,
    values_ref, right_ref, left_ref, up_ref, down_ref,
    faces_ref, neighbours, features, cotangent, active, send_ref, sems,
):
    pairs = (
        (neighbours_any, neighbours), (features_any, features), (cotangent_any, cotangent),
        (active_any, active),
    )
    copies = [pltpu.make_async_copy(s, d, sems.at[t]) for t, (s, d) in enumerate(pairs)]
    for copy in copies:
        copy.start()
    for copy in copies:
        copy.wait()
    choose_sends(neighbours, send_ref)
    for b in range(4):
        mask = active[b : b + 1, :].astype(F32)
        f = features[b].astype(F32)
        values_ref[b * 64 : b * 64 + 64, :] = (mask * (f / (1.0 + jnp.exp(-f)))).astype(BF)
        values_ref[256 + b * 64 : 320 + b * 64, :] = (mask * cotangent[b].astype(F32)).astype(BF)
    own_faces(values_ref, faces_ref)
    low = low_half((64, 128))
    pack(
        send_ref,
        lambda ids: [jnp.where(low, faces_ref[0, i], faces_ref[1, i]) for i in ids],
        right_ref, left_ref, up_ref, down_ref,
    )


def as_column(row):
    here = lax.broadcasted_iota(jnp.int32, (64, 64), 0)
    there = lax.broadcasted_iota(jnp.int32, (64, 64), 1)
    picked = jnp.where(here == there, jnp.broadcast_to(row, (64, 64)), 0.0)
    return jnp.broadcast_to(jnp.sum(picked, axis=1, keepdims=True), (64, 128))


def prepare_kernel(
    values, active, first, second, scale, shift,
    faces_ref, mask_ref, w_first, w_back, gain_ref, shift_ref, e_yz, e_x, windows,
):
    own_faces(values, faces_ref)
    mask_ref[...] = active[...].astype(F32)
    e_yz[...], e_x[...], windows[...] = yz_matrix(), x_matrix(), window_matrix()
    gain_ref[...] = 1.0 + as_column(scale[...])
    shift_ref[...] = as_column(shift[...])
    for i in range(3):
        for jl in range(9):
            k = 9 * i + jl
            rows, lanes = slice(i * 64, i * 64 + 64), slice(jl * 64, jl * 64 + 64)
            w_first[rows, lanes] = first[k]
            w_back[rows, lanes] = second[26 - k].T


def fill_table(table, faces, arrays, groups):
    low = low_half((64, 128))
    for a in range(arrays):
        for f in range(24):
            table[a, f] = faces[a, f] if arrays == 2 else faces[f]
        table[a, ZERO_ROW] = jnp.zeros((64, 128), BF)
    for ref, base, count in groups:
        for t in range(count * arrays // 2):
            tile = ref[t]
            swapped = jnp.concatenate([tile[:, 64:], tile[:, :64]], axis=1)
            first, second = jnp.where(low, tile, swapped), jnp.where(low, swapped, tile)
            if arrays == 2:
                table[0, base + t], table[1, base + t] = first, second
            else:
                table[0, base + 2 * t], table[0, base + 2 * t + 1] = first, second


def build_padded(index_ref, table, values, ext, side_yz, side_x, e_yz, e_x, arrays):
    lane = lax.broadcasted_iota(jnp.int32, (64, 128), 1)
    low, u_far, v_far = lane < 64, (lane & 32) != 0, (lane & 4) != 0
    for a in range(arrays):
        for b in range(4):
            row = (a * 4 + b) * 64

            def face(*offset):
                return table[a, index_ref[b * 26 + DIRECTIONS.index(offset)]]

            def both(low_face, high_face):
                return jnp.where(low, low_face, high_face)

            def along_v(u, v, make):
                if v is None:
                    return jnp.where(v_far, make(u, -1), make(u, 1))
                return make(u, v)

            def tile(u, v, make):
                if u is None:
                    return jnp.where(u_far, along_v(-1, v, make), along_v(1, v, make))
                return along_v(u, v, make)

            def x_faces(y, z):
                return both(face(1, y, z), face(-1, y, z))

            for t, (y, z) in enumerate(X_TILES):
                side_x[row : row + 64, t * 128 : t * 128 + 128] = tile(y, z, x_faces)

            def y_faces(_, z):
                return both(face(0, 1, z), face(0, -1, z))

            for t, (_, z) in enumerate(Y_TILES):
                side_yz[row : row + 64, t * 128 : t * 128 + 128] = along_v(0, z, y_faces)
            side_yz[row : row + 64, 256:384] = both(face(0, 0, 1), face(0, 0, -1))
    outer = dot(side_x[...], e_x[...]).astype(BF)
    ext[:, 0:128] = outer[:, 0:128]
    ext[:, 1152:1280] = outer[:, 128:256]
    for m in range(4):
        known = jnp.concatenate([side_yz[...], values[:, m * 128 : m * 128 + 128]], axis=1)
        inner = dot(known, e_yz[:, m * 256 : m * 256 + 256])
        ext[:, 128 + m * 256 : 384 + m * 256] = inner.astype(BF)


def columns(ext, windows, cols):
    for m in range(5):
        moved = dot(ext[:, m * 256 : m * 256 + 256], windows[...]).astype(BF)
        for a, col in enumerate(cols):
            for b in range(4):
                row = (a * 4 + b) * 64
                lane = b * 640 + m * 128
                for k in range(9):
                    col[k * 64 : k * 64 + 64, lane : lane + 128] = moved[
                        row : row + 64, k * 128 : k * 128 + 128
                    ]


def three_planes(product, lane):
    return (
        product[0:64, lane : lane + 512]
        + product[64:128, lane + 64 : lane + 576]
        + product[128:192, lane + 128 : lane + 640]
    )


def stack_planes(stack, lane, values):
    none = jnp.zeros((64, 64), BF)
    wide = jnp.zeros((64, 128), BF)
    stack[0:64, lane : lane + 640] = jnp.concatenate([values, wide], axis=1)
    stack[64:128, lane : lane + 640] = jnp.concatenate([none, values, none], axis=1)
    stack[128:192, lane : lane + 640] = jnp.concatenate([wide, values], axis=1)


def second_kernel(
    index_ref, values, faces, from_left, from_right, from_up, from_down, mask_ref,
    w_first, w_back, gain_ref, shift_ref, e_yz, e_x, windows,
    hidden_ref, sums_any,
    table, ext, side_yz, side_x, col_a, col_s, stack_h, stack_s, sums_ref, sems,
):
    copies = []

    def send(start, stop, t):
        rows = pl.ds(start, stop - start)
        copies.append(pltpu.make_async_copy(sums_ref.at[rows], sums_any.at[rows], sems.at[t]))
        copies[-1].start()

    sums_ref[1728:2048, :] = jnp.zeros((320, 128), BF)
    send(1728, 2048, 0)
    groups = ((from_left, 24, 4), (from_right, 28, 4), (from_up, 32, 6), (from_down, 38, 6))
    fill_table(table, faces, 2, groups)
    build_padded(index_ref, table, values, ext, side_yz, side_x, e_yz, e_x, 2)
    columns(ext, windows, (col_a, col_s))
    gain = gain_ref[:, 0:1]
    shift = shift_ref[:, 0:1]
    for pair in range(2):
        these = slice(pair * 1280, pair * 1280 + 1280)
        first = dot(w_first[...], col_a[:, these])
        second = dot(w_back[...], col_s[:, these])
        for half in range(2):
            b = 2 * pair + half
            pre, back = three_planes(first, half * 640), three_planes(second, half * 640)
            mask = mask_ref[b : b + 1, :]
            shaped = pre * gain + shift
            gate = 1.0 / (1.0 + jnp.exp(-shaped))
            hidden = (mask * (shaped * gate)).astype(BF)
            slope = (back * mask * gate * (1.0 + shaped * (1.0 - gate)) * gain).astype(BF)
            hidden_ref[b * 64 : b * 64 + 64, :] = hidden
            stack_planes(stack_h, b * 640, hidden)
            stack_planes(stack_s, b * 640, slope)
    pack_sums(dot_nt(col_s[...], stack_h[...]), sums_ref, 0)
    send(0, 864, 1)
    pack_sums(dot_nt(col_a[...], stack_s[...]), sums_ref, 864)
    send(864, 1728, 2)
    for copy in copies:
        copy.wait()


def faces_kernel(
    send_ref, hidden,
    hidden_faces, right_ref, left_ref, up_ref, down_ref,
):
    out = dot(hidden[...], face_matrix()).astype(BF)
    for b in range(4):
        for f in range(6):
            hidden_faces[b * 6 + f] = out[b * 64 : b * 64 + 64, f * 128 : f * 128 + 128]
    low = low_half((64, 128))
    pack(
        send_ref,
        lambda ids: [
            jnp.where(low, hidden_faces[i], hidden_faces[j]) for i, j in zip(ids[::2], ids[1::2])
        ],
        right_ref, left_ref, up_ref, down_ref,
    )


def pack_sums(total, sums_ref, base):
    sums_ref[base : base + 576, :] = total[:, 0:128].astype(BF)
    sums_ref[base + 576 : base + 864, :] = jnp.concatenate(
        [total[0:288, 128:192], total[288:576, 128:192]], axis=1
    ).astype(BF)


def third_kernel(
    index_ref, hidden_faces, from_left, from_right, from_up, from_down, hidden,
    active, features, weight,
    out_ref,
    table, ext, side_yz, side_x, col, w_second, e_yz, e_x, windows,
):
    e_yz[...], e_x[...], windows[...] = yz_matrix(), x_matrix(), window_matrix()
    for i in range(3):
        for jl in range(9):
            w_second[i * 64 : i * 64 + 64, jl * 64 : jl * 64 + 64] = weight[9 * i + jl]
    groups = ((from_left, 24, 4), (from_right, 28, 4), (from_up, 32, 6), (from_down, 38, 6))
    fill_table(table, hidden_faces, 1, groups)
    build_padded(index_ref, table, hidden, ext, side_yz, side_x, e_yz, e_x, 1)
    columns(ext, windows, (col,))
    for pair in range(2):
        product = dot(w_second[...], col[:, pair * 1280 : pair * 1280 + 1280])
        for half in range(2):
            b = 2 * pair + half
            second = active[b : b + 1, :].astype(F32) * three_planes(product, half * 640)
            out_ref[b] = (features[b].astype(F32) + second).astype(BF)


def share_kernel(parts, left_any, right_any, out_ref):
    totals = [parts[d].astype(F32) for d in range(4)]
    for d in range(4, 128):
        totals[d % 4] = totals[d % 4] + parts[d].astype(F32)
    total = ((totals[0] + totals[1]) + (totals[2] + totals[3])).astype(BF)
    for d in range(128):
        out_ref[d] = total


def unpack_kernel(sums, first_any, second_any, first, second, sems):
    copies = []
    for t, (grad, grad_any) in enumerate(((second, second_any), (first, first_any))):
        base = t * 864
        for i in range(3):
            for jl in range(9):
                if i < 2:
                    block = sums[base + jl * 64 : base + jl * 64 + 64, i * 64 : i * 64 + 64]
                else:
                    pieces = []
                    for r in (jl * 64, jl * 64 + 32):
                        lane, at = (0, r) if r < 288 else (64, r - 288)
                        at += base + 576
                        pieces.append(sums[at : at + 32, lane : lane + 64])
                    block = jnp.concatenate(pieces, axis=0)
                block = block.astype(F32)
                k = 9 * i + jl
                if t == 0:
                    grad[26 - k] = block
                else:
                    grad[k] = block.T
            nine = pl.ds(18 - 9 * i if t == 0 else 9 * i, 9)
            copies.append(
                pltpu.make_async_copy(grad.at[nine], grad_any.at[nine], sems.at[3 * t + i])
            )
            copies[-1].start()
    for copy in copies:
        copy.wait()


def sent(array, step):
    pairs = []
    for i in range(32):
        j = i + step
        if 0 <= j < 32 and (abs(step) == GRID_X or i // GRID_X == j // GRID_X):
            pairs.append((i, j))
    return lax.ppermute(array, "brick", pairs)


def forward_kernel(from_left, from_right, up, down, after_any, up_ref, down_ref):
    n = up.shape[0]
    up_ref[0:n] = up[...]
    down_ref[0:n] = down[...]
    for t, ref in enumerate((from_left, from_right)):
        up_ref[n + t * n : 2 * n + t * n] = ref[3 * n :]
        down_ref[n + t * n : 2 * n + t * n] = ref[2 * n : 3 * n]


def first_round(right, left):
    return sent(right, 1), sent(left, -1)


def second_round(from_left, from_right, up, down, after):
    upward, downward = call(
        forward_kernel,
        [(VMEM, t) for t in (from_left, from_right, up, down)] + [(ANY, after)],
        [(VMEM, shape((3 * up.shape[0], 64, 128)))] * 2,
        [],
        8,
        0,
    )
    return from_left, from_right, sent(upward, GRID_X), sent(downward, -GRID_X)


def shape(dims, dtype=BF):
    return jax.ShapeDtypeStruct(dims, dtype)


SMEM = pl.BlockSpec(memory_space=pltpu.SMEM)
VMEM = pl.BlockSpec(memory_space=pltpu.VMEM)
ANY = pl.BlockSpec(memory_space=pl.ANY)
HBM = pl.BlockSpec(memory_space=pltpu.HBM)


def call(kernel, operands, outs, scratch, limit, us):
    return pl.pallas_call(
        kernel,
        out_shape=tuple(o for _, o in outs),
        in_specs=[s for s, _ in operands],
        out_specs=tuple(s for s, _ in outs),
        scratch_shapes=scratch,
        compiler_params=pltpu.CompilerParams(vmem_limit_bytes=limit << 20),
        cost_estimate=pl.CostEstimate(flops=us * 10**9, bytes_accessed=0, transcendentals=0),
        name=kernel.__name__,
    )(*(o for _, o in operands))


def shards(
    features, active, neighbours, first_weight, second_weight, film_scale, film_shift, cotangent
):
    def messages(arrays):
        return [(VMEM, shape((n * arrays, 64, 128))) for n in (4, 4, 1, 1)]


    values, *outgoing = call(
        first_kernel,
        [(HBM, t) for t in (neighbours, features, cotangent, active)],
        [(VMEM, shape((512, 512)))] + messages(2),
        [
            pltpu.VMEM((2, 24, 64, 128), BF),
            pltpu.SMEM((4, 26), jnp.int32),
            pltpu.VMEM((4, 64, 512), BF),
            pltpu.VMEM((4, 64, 512), BF),
            pltpu.VMEM((4, 512), jnp.int32),
            pltpu.SMEM((288,), jnp.int32),
            pltpu.SemaphoreType.DMA((4,)),
        ],
        56,
        4,
    )
    arrived = second_round(*first_round(*outgoing[:2]), *outgoing[2:], outgoing[2])
    index, send_ids = call(
        tables_kernel,
        [(HBM, neighbours), (ANY, arrived[0])],
        [(SMEM, shape((104,), jnp.int32)), (SMEM, shape((288,), jnp.int32))],
        [
            pltpu.SMEM((4, 26), jnp.int32),
            pltpu.SMEM((10,), jnp.int32),
            pltpu.SMEM((240,), jnp.int32),
            pltpu.SemaphoreType.DMA,
        ],
        8,
        3,
    )
    spread_shapes = [(512, 1024), (512, 256), (256, 1152)]
    prepared = call(
        prepare_kernel,
        [
            (VMEM, t)
            for t in (
                values,
                active,
                first_weight,
                second_weight,
                film_scale.reshape(1, 64),
                film_shift.reshape(1, 64),
            )
        ],
        [(VMEM, shape((2, 24, 64, 128))), (VMEM, shape((4, 512), F32))]
        + [(VMEM, shape((192, 576)))] * 2
        + [(VMEM, shape((64, 128), F32))] * 2
        + [(VMEM, shape(dims)) for dims in spread_shapes],
        [],
        16,
        3,
    )
    faces, mask, w_first, w_back, gain, shift, *spreads = prepared

    hidden, sums = call(
        second_kernel,
        [(SMEM, index)]
        + [(VMEM, t) for t in (values, faces, *arrived, mask, w_first, w_back, gain, shift)]
        + [(VMEM, t) for t in spreads],
        [
            (VMEM, shape((256, 512))),
            (ANY, shape((2048, 128))),
        ],
        [
            pltpu.VMEM((2, 45, 64, 128), BF),
            pltpu.VMEM((512, 1280), BF),
            pltpu.VMEM((512, 384), BF),
            pltpu.VMEM((512, 512), BF),
            pltpu.VMEM((576, 2560), BF),
            pltpu.VMEM((576, 2560), BF),
            pltpu.VMEM((192, 2560), BF),
            pltpu.VMEM((192, 2560), BF),
            pltpu.VMEM((2048, 128), BF),
            pltpu.SemaphoreType.DMA((3,)),
        ],
        32,
        10,
    )
    parts = lax.all_to_all(sums.reshape(128, 16, 128), AXES, 0, 0, tiled=True)
    hidden_faces, *outgoing = call(
        faces_kernel,
        [(SMEM, send_ids), (VMEM, hidden)],
        [(VMEM, shape((24, 64, 128)))] + messages(1),
        [],
        16,
        8,
    )
    sides = first_round(*outgoing[:2])
    (shares,) = call(
        share_kernel, [(VMEM, parts)] + [(ANY, t) for t in sides], [(VMEM, shape((128, 16, 128)))], [], 16, 1
    )
    arrived = second_round(*sides, *outgoing[2:], shares)
    sums = lax.all_to_all(shares, AXES, 0, 0, tiled=True)
    (block_output,) = call(
        third_kernel,
        [(SMEM, index)]
        + [(VMEM, t) for t in (hidden_faces, *arrived, hidden, active, features, second_weight)],
        [(VMEM, shape((4, 64, 512)))],
        [
            pltpu.VMEM((1, 45, 64, 128), BF),
            pltpu.VMEM((256, 1280), BF),
            pltpu.VMEM((256, 384), BF),
            pltpu.VMEM((256, 512), BF),
            pltpu.VMEM((576, 2560), BF),
            pltpu.VMEM((192, 576), BF),
        ]
        + [pltpu.VMEM(dims, BF) for dims in spread_shapes],
        16,
        2,
    )
    grad_first, grad_second = call(
        unpack_kernel,
        [(VMEM, sums.reshape(2048, 128))],
        [(ANY, shape((27, 64, 64), F32))] * 2,
        [
            pltpu.VMEM((27, 64, 64), F32),
            pltpu.VMEM((27, 64, 64), F32),
            pltpu.SemaphoreType.DMA((6,)),
        ],
        16,
        0,
    )
    return block_output, grad_first, grad_second


def solution(mesh):
    split = P(AXES, None, None)
    rows = P(AXES, None)
    return jax.shard_map(
        shards,
        mesh=mesh,
        in_specs=(split, rows, rows, P(), P(), P(), P(), split),
        out_specs=(split, P(), P()),
        check_vma=False,
    )
```

```python
import jax
import jax.numpy as jnp
from jax import lax
from jax.experimental import pallas as pl
from jax.experimental.pallas import tpu as pltpu
from jax.sharding import PartitionSpec as P

AXES = ("region", "brick")
GRID_X = 8
ZERO_ROW = 44
ARRIVALS = {
    (-1, 0): (24, 4),
    (1, 0): (28, 4),
    (0, -1): (32, 2),
    (-1, -1): (34, 2),
    (1, -1): (36, 2),
    (0, 1): (38, 2),
    (-1, 1): (40, 2),
    (1, 1): (42, 2),
}
BF = jnp.bfloat16
F32 = jnp.float32


def direction_list():
    return [
        (a, b, c)
        for a in (-1, 0, 1)
        for b in (-1, 0, 1)
        for c in (-1, 0, 1)
        if (a, b, c) != (0, 0, 0)
    ]


DIRECTIONS = direction_list()


def face_of(vector):
    if vector[0] != 0:
        return 0 if vector[0] < 0 else 1
    if vector[1] != 0:
        return 2 if vector[1] < 0 else 3
    return 4 if vector[2] < 0 else 5


SEND_FACE = [face_of(d) for d in DIRECTIONS]
READ_FACE = [face_of(tuple(-t for t in d)) for d in DIRECTIONS]


X_TILES = [(0, 0), (0, None), (None, 0), (None, None)]
Y_TILES = [(0, 0), (0, None)]


def one_hot(rows, source):
    at = lax.broadcasted_iota(jnp.int32, (rows, source.shape[1]), 0)
    return jnp.where(at == source, 1.0, 0.0).astype(BF)


def lanes(count):
    return lax.broadcasted_iota(jnp.int32, (1, count), 1)


def face_matrix():
    lane = lanes(768)
    face, u, v = lane >> 7, (lane >> 3) & 7, lane & 7
    first = jnp.where(face < 2, u * 8 + v, jnp.where(face < 4, u * 64 + v, u * 64 + v * 8))
    far = jnp.where(face == 1, 448, jnp.where(face == 3, 56, jnp.where(face == 5, 7, 0)))
    return one_hot(512, first + far)


def padded_lane(count):
    lane = lanes(count)
    cell = lane & 127
    y = (cell * 205) >> 11
    return lane >> 7, y, cell - y * 10


def window_matrix():
    lane = lanes(1152)
    tap, plane, y, z = lane >> 7, (lane >> 6) & 1, (lane >> 3) & 7, lane & 7
    j = jnp.where(tap < 3, 0, jnp.where(tap < 6, 1, 2))
    return one_hot(256, plane * 128 + (y + j) * 10 + z + tap - 3 * j)


def yz_matrix():
    x, y, z = padded_lane(1024)
    y_edge, z_edge = (y == 0) | (y == 9), (z == 0) | (z == 9)
    z_cell = jnp.where(z == 0, 7, jnp.where(z == 9, 0, z - 1))
    from_y = jnp.where(z_edge, 128, 0) + jnp.where(y == 0, 64, 0) + x * 8 + z_cell
    from_z = 256 + jnp.where(z == 0, 64, 0) + x * 8 + y - 1
    own = 384 + (x & 1) * 64 + (y - 1) * 8 + z - 1
    source = jnp.where(y_edge, from_y, jnp.where(z_edge, from_z, own))
    return one_hot(512, jnp.where(y < 10, source, -1))


def x_matrix():
    side, y, z = padded_lane(256)
    y_edge, z_edge = (y == 0) | (y == 9), (z == 0) | (z == 9)
    y_cell = jnp.where(y == 0, 7, jnp.where(y == 9, 0, y - 1))
    z_cell = jnp.where(z == 0, 7, jnp.where(z == 9, 0, z - 1))
    tile = jnp.where(y_edge, 256, 0) + jnp.where(z_edge, 128, 0)
    source = tile + jnp.where(side == 0, 64, 0) + y_cell * 8 + z_cell
    return one_hot(512, jnp.where(y < 10, source, -1))


def dot(a, b):
    return lax.dot_general(a, b, (((1,), (0,)), ((), ())), preferred_element_type=F32)


def dot_nt(a, b):
    return lax.dot_general(a, b, (((1,), (1,)), ((), ())), preferred_element_type=F32)


def low_half(shape):
    return lax.broadcasted_iota(jnp.int32, shape, len(shape) - 1) < 64


def place(n, origin):
    return jnp.where(n >= 0, ((n >> 5) & 3) * 3 + ((n >> 2) & 7) + origin, 9)


def own_origin():
    mine = lax.axis_index("brick")
    return 4 - (mine >> 3) * 3 - (mine & 7)


def choose_sends(neighbours, send_ref, seen=None):
    origin = own_origin()
    readers = []
    for b in range(4):
        bits = [0] * 6
        for e in range(26):
            n = neighbours[b, e]
            where = place(n, origin)
            bits[SEND_FACE[e]] = bits[SEND_FACE[e]] | jnp.left_shift(1, where)
            if seen is not None:
                seen(b, e, n, where)
        readers += bits
    for x, y in ARRIVALS:
        s = (y + 1) * 3 + x + 1
        for t in range(4):
            send_ref[s * 32 + t] = 0
        sent = s * 32
        for f in range(24):
            send_ref[sent] = f
            sent = sent + ((readers[f] >> s) & 1)


def tables_kernel(
    neighbours_any, after_any, index_ref, send_ref, neighbours, held, rank_ref, sem
):
    copy = pltpu.make_async_copy(neighbours_any, neighbours, sem)
    copy.start()
    for s in range(10):
        held[s] = 0
    for f in range(24):
        rank_ref[4 * 24 + f] = f
        rank_ref[9 * 24 + f] = ZERO_ROW
    rows = {}

    def mark(b, e, n, where):
        face = (n & 3) * 6 + READ_FACE[e]
        rows[b, e] = where * 24 + face
        held[where] = held[where] | jnp.left_shift(1, face)

    copy.wait()
    choose_sends(neighbours, send_ref, mark)
    for (x, y), (base, count) in ARRIVALS.items():
        s = (y + 1) * 3 + x + 1
        bits = held[s]
        got = base
        for f in range(24):
            rank_ref[s * 24 + f] = jnp.minimum(got, base + count - 1)
            got = got + ((bits >> f) & 1)
    for (b, e), row in rows.items():
        index_ref[b * 26 + e] = rank_ref[row]


def send_slots(send_ref, x, y):
    s = (y + 1) * 3 + x + 1
    return [send_ref[s * 32 + t] for t in range(4 if y == 0 else 2)]


def pack(send_ref, tiles_of, right_ref, left_ref, up_ref, down_ref):
    for ref, x in ((right_ref, 1), (left_ref, -1)):
        ids = send_slots(send_ref, x, 0) + send_slots(send_ref, x, -1) + send_slots(send_ref, x, 1)
        for t, tile in enumerate(tiles_of(ids)):
            ref[t] = tile
    for ref, y in ((up_ref, 1), (down_ref, -1)):
        for t, tile in enumerate(tiles_of(send_slots(send_ref, 0, y))):
            ref[t] = tile


def own_faces(values, matrix, faces_ref):
    faces = dot(values[...], matrix).astype(BF)
    for a in range(2):
        for b in range(4):
            for f in range(6):
                row = (a * 4 + b) * 64
                faces_ref[a, b * 6 + f] = faces[row : row + 64, f * 128 : f * 128 + 128]


def first_kernel(
    neighbours_any, features_any, cotangent_any, active_any,
    values_ref, right_ref, left_ref, up_ref, down_ref,
    faces_ref, face_mat, neighbours, features, cotangent, active, send_ref, sems,
):
    pairs = (
        (neighbours_any, neighbours), (features_any, features), (cotangent_any, cotangent),
        (active_any, active),
    )
    copies = [pltpu.make_async_copy(s, d, sems.at[t]) for t, (s, d) in enumerate(pairs)]
    for copy in copies:
        copy.start()
    face_mat[...] = face_matrix()
    for copy in copies:
        copy.wait()
    choose_sends(neighbours, send_ref)
    for b in range(4):
        mask = active[b : b + 1, :].astype(F32)
        f = features[b].astype(F32)
        values_ref[b * 64 : b * 64 + 64, :] = (mask * (f / (1.0 + jnp.exp(-f)))).astype(BF)
        values_ref[256 + b * 64 : 320 + b * 64, :] = (mask * cotangent[b].astype(F32)).astype(BF)
    own_faces(values_ref, face_mat[...], faces_ref)
    low = low_half((64, 128))
    pack(
        send_ref,
        lambda ids: [jnp.where(low, faces_ref[0, i], faces_ref[1, i]) for i in ids],
        right_ref, left_ref, up_ref, down_ref,
    )


def as_column(row):
    here = lax.broadcasted_iota(jnp.int32, (64, 64), 0)
    there = lax.broadcasted_iota(jnp.int32, (64, 64), 1)
    picked = jnp.where(here == there, jnp.broadcast_to(row, (64, 64)), 0.0)
    return jnp.broadcast_to(jnp.sum(picked, axis=1, keepdims=True), (64, 128))


def prepare_kernel(
    values, active, first, second, scale, shift,
    faces_ref, mask_ref, w_first, w_back, gain_ref, shift_ref, e_yz, e_x, windows,
):
    own_faces(values, face_matrix(), faces_ref)
    mask_ref[...] = active[...].astype(F32)
    e_yz[...], e_x[...], windows[...] = yz_matrix(), x_matrix(), window_matrix()
    gain_ref[...] = 1.0 + as_column(scale[...])
    shift_ref[...] = as_column(shift[...])
    for i in range(3):
        for jl in range(9):
            k = 9 * i + jl
            rows, lanes = slice(i * 64, i * 64 + 64), slice(jl * 64, jl * 64 + 64)
            w_first[rows, lanes] = first[k]
            w_back[rows, lanes] = second[26 - k].T


def fill_table(table, faces, arrays, groups):
    low = low_half((64, 128))
    for a in range(arrays):
        for f in range(24):
            table[a, f] = faces[a, f] if arrays == 2 else faces[f]
        table[a, ZERO_ROW] = jnp.zeros((64, 128), BF)
    for ref, base, count in groups:
        for t in range(count * arrays // 2):
            tile = ref[t]
            swapped = jnp.concatenate([tile[:, 64:], tile[:, :64]], axis=1)
            first, second = jnp.where(low, tile, swapped), jnp.where(low, swapped, tile)
            if arrays == 2:
                table[0, base + t], table[1, base + t] = first, second
            else:
                table[0, base + 2 * t], table[0, base + 2 * t + 1] = first, second


def build_padded(index_ref, table, values, ext, side_yz, side_x, e_yz, e_x, arrays):
    lane = lax.broadcasted_iota(jnp.int32, (64, 128), 1)
    low, u_far, v_far = lane < 64, (lane & 32) != 0, (lane & 4) != 0
    for a in range(arrays):
        for b in range(4):
            row = (a * 4 + b) * 64

            def face(*offset):
                return table[a, index_ref[b * 26 + DIRECTIONS.index(offset)]]

            def both(low_face, high_face):
                return jnp.where(low, low_face, high_face)

            def along_v(u, v, make):
                if v is None:
                    return jnp.where(v_far, make(u, -1), make(u, 1))
                return make(u, v)

            def tile(u, v, make):
                if u is None:
                    return jnp.where(u_far, along_v(-1, v, make), along_v(1, v, make))
                return along_v(u, v, make)

            def x_faces(y, z):
                return both(face(1, y, z), face(-1, y, z))

            for t, (y, z) in enumerate(X_TILES):
                side_x[row : row + 64, t * 128 : t * 128 + 128] = tile(y, z, x_faces)

            def y_faces(_, z):
                return both(face(0, 1, z), face(0, -1, z))

            for t, (_, z) in enumerate(Y_TILES):
                side_yz[row : row + 64, t * 128 : t * 128 + 128] = along_v(0, z, y_faces)
            side_yz[row : row + 64, 256:384] = both(face(0, 0, 1), face(0, 0, -1))
    outer = dot(side_x[...], e_x[...]).astype(BF)
    ext[:, 0:128] = outer[:, 0:128]
    ext[:, 1152:1280] = outer[:, 128:256]
    for m in range(4):
        known = jnp.concatenate([side_yz[...], values[:, m * 128 : m * 128 + 128]], axis=1)
        inner = dot(known, e_yz[:, m * 256 : m * 256 + 256])
        ext[:, 128 + m * 256 : 384 + m * 256] = inner.astype(BF)


def columns(ext, windows, cols):
    for m in range(5):
        moved = dot(ext[:, m * 256 : m * 256 + 256], windows[...]).astype(BF)
        for a, col in enumerate(cols):
            for b in range(4):
                row = (a * 4 + b) * 64
                lane = b * 640 + m * 128
                for k in range(9):
                    col[k * 64 : k * 64 + 64, lane : lane + 128] = moved[
                        row : row + 64, k * 128 : k * 128 + 128
                    ]


def three_planes(product, lane):
    return (
        product[0:64, lane : lane + 512]
        + product[64:128, lane + 64 : lane + 576]
        + product[128:192, lane + 128 : lane + 640]
    )


def stack_planes(stack, lane, values):
    none = jnp.zeros((64, 64), BF)
    wide = jnp.zeros((64, 128), BF)
    stack[0:64, lane : lane + 640] = jnp.concatenate([values, wide], axis=1)
    stack[64:128, lane : lane + 640] = jnp.concatenate([none, values, none], axis=1)
    stack[128:192, lane : lane + 640] = jnp.concatenate([wide, values], axis=1)


def second_kernel(
    index_ref, values, faces, from_left, from_right, from_up, from_down, mask_ref,
    w_first, w_back, gain_ref, shift_ref, e_yz, e_x, windows,
    hidden_ref, sums_any,
    table, ext, side_yz, side_x, col_a, col_s, stack_h, stack_s, sums_ref, sems,
):
    copies = []

    def send(start, stop, t):
        rows = pl.ds(start, stop - start)
        copies.append(pltpu.make_async_copy(sums_ref.at[rows], sums_any.at[rows], sems.at[t]))
        copies[-1].start()

    sums_ref[1728:2048, :] = jnp.zeros((320, 128), BF)
    send(1728, 2048, 0)
    groups = ((from_left, 24, 4), (from_right, 28, 4), (from_up, 32, 6), (from_down, 38, 6))
    fill_table(table, faces, 2, groups)
    build_padded(index_ref, table, values, ext, side_yz, side_x, e_yz, e_x, 2)
    columns(ext, windows, (col_a, col_s))
    gain = gain_ref[:, 0:1]
    shift = shift_ref[:, 0:1]
    for pair in range(2):
        these = slice(pair * 1280, pair * 1280 + 1280)
        first = dot(w_first[...], col_a[:, these])
        second = dot(w_back[...], col_s[:, these])
        for half in range(2):
            b = 2 * pair + half
            pre, back = three_planes(first, half * 640), three_planes(second, half * 640)
            mask = mask_ref[b : b + 1, :]
            shaped = pre * gain + shift
            gate = 1.0 / (1.0 + jnp.exp(-shaped))
            hidden = (mask * (shaped * gate)).astype(BF)
            slope = (back * mask * gate * (1.0 + shaped * (1.0 - gate)) * gain).astype(BF)
            hidden_ref[b * 64 : b * 64 + 64, :] = hidden
            stack_planes(stack_h, b * 640, hidden)
            stack_planes(stack_s, b * 640, slope)
    pack_sums(dot_nt(col_s[...], stack_h[...]), sums_ref, 0)
    send(0, 864, 1)
    pack_sums(dot_nt(col_a[...], stack_s[...]), sums_ref, 864)
    send(864, 1728, 2)
    for copy in copies:
        copy.wait()


def faces_kernel(
    send_ref, hidden,
    hidden_faces, right_ref, left_ref, up_ref, down_ref,
):
    out = dot(hidden[...], face_matrix()).astype(BF)
    for b in range(4):
        for f in range(6):
            hidden_faces[b * 6 + f] = out[b * 64 : b * 64 + 64, f * 128 : f * 128 + 128]
    low = low_half((64, 128))
    pack(
        send_ref,
        lambda ids: [
            jnp.where(low, hidden_faces[i], hidden_faces[j]) for i, j in zip(ids[::2], ids[1::2])
        ],
        right_ref, left_ref, up_ref, down_ref,
    )


def pack_sums(total, sums_ref, base):
    sums_ref[base : base + 576, :] = total[:, 0:128].astype(BF)
    sums_ref[base + 576 : base + 864, :] = jnp.concatenate(
        [total[0:288, 128:192], total[288:576, 128:192]], axis=1
    ).astype(BF)


def third_kernel(
    index_ref, hidden_faces, from_left, from_right, from_up, from_down, hidden,
    active, features, weight,
    out_ref,
    table, ext, side_yz, side_x, col, w_second, e_yz, e_x, windows,
):
    e_yz[...], e_x[...], windows[...] = yz_matrix(), x_matrix(), window_matrix()
    for i in range(3):
        for jl in range(9):
            w_second[i * 64 : i * 64 + 64, jl * 64 : jl * 64 + 64] = weight[9 * i + jl]
    groups = ((from_left, 24, 4), (from_right, 28, 4), (from_up, 32, 6), (from_down, 38, 6))
    fill_table(table, hidden_faces, 1, groups)
    build_padded(index_ref, table, hidden, ext, side_yz, side_x, e_yz, e_x, 1)
    columns(ext, windows, (col,))
    for pair in range(2):
        product = dot(w_second[...], col[:, pair * 1280 : pair * 1280 + 1280])
        for half in range(2):
            b = 2 * pair + half
            second = active[b : b + 1, :].astype(F32) * three_planes(product, half * 640)
            out_ref[b] = (features[b].astype(F32) + second).astype(BF)


def share_kernel(parts, left_any, right_any, out_ref):
    totals = [parts[d].astype(F32) for d in range(4)]
    for d in range(4, 128):
        totals[d % 4] = totals[d % 4] + parts[d].astype(F32)
    total = ((totals[0] + totals[1]) + (totals[2] + totals[3])).astype(BF)
    for d in range(128):
        out_ref[d] = total


def unpack_kernel(sums, first_any, second_any, first, second, sems):
    copies = []
    for t, (grad, grad_any) in enumerate(((second, second_any), (first, first_any))):
        base = t * 864
        for i in range(3):
            for jl in range(9):
                if i < 2:
                    block = sums[base + jl * 64 : base + jl * 64 + 64, i * 64 : i * 64 + 64]
                else:
                    pieces = []
                    for r in (jl * 64, jl * 64 + 32):
                        lane, at = (0, r) if r < 288 else (64, r - 288)
                        at += base + 576
                        pieces.append(sums[at : at + 32, lane : lane + 64])
                    block = jnp.concatenate(pieces, axis=0)
                block = block.astype(F32)
                k = 9 * i + jl
                if t == 0:
                    grad[26 - k] = block
                else:
                    grad[k] = block.T
            nine = pl.ds(18 - 9 * i if t == 0 else 9 * i, 9)
            copies.append(
                pltpu.make_async_copy(grad.at[nine], grad_any.at[nine], sems.at[3 * t + i])
            )
            copies[-1].start()
    for copy in copies:
        copy.wait()


def sent(array, step):
    pairs = []
    for i in range(32):
        j = i + step
        if 0 <= j < 32 and (abs(step) == GRID_X or i // GRID_X == j // GRID_X):
            pairs.append((i, j))
    return lax.ppermute(array, "brick", pairs)


def forward_kernel(from_left, from_right, up, down, after_any, up_ref, down_ref):
    n = up.shape[0]
    up_ref[0:n] = up[...]
    down_ref[0:n] = down[...]
    for t, ref in enumerate((from_left, from_right)):
        up_ref[n + t * n : 2 * n + t * n] = ref[3 * n :]
        down_ref[n + t * n : 2 * n + t * n] = ref[2 * n : 3 * n]


def first_round(right, left):
    return sent(right, 1), sent(left, -1)


def second_round(from_left, from_right, up, down, after):
    upward, downward = call(
        forward_kernel,
        [(VMEM, t) for t in (from_left, from_right, up, down)] + [(ANY, after)],
        [(VMEM, shape((3 * up.shape[0], 64, 128)))] * 2,
        [],
        8,
        0,
    )
    return from_left, from_right, sent(upward, GRID_X), sent(downward, -GRID_X)


def shape(dims, dtype=BF):
    return jax.ShapeDtypeStruct(dims, dtype)


SMEM = pl.BlockSpec(memory_space=pltpu.SMEM)
VMEM = pl.BlockSpec(memory_space=pltpu.VMEM)
ANY = pl.BlockSpec(memory_space=pl.ANY)
HBM = pl.BlockSpec(memory_space=pltpu.HBM)


def call(kernel, operands, outs, scratch, limit, us):
    return pl.pallas_call(
        kernel,
        out_shape=tuple(o for _, o in outs),
        in_specs=[s for s, _ in operands],
        out_specs=tuple(s for s, _ in outs),
        scratch_shapes=scratch,
        compiler_params=pltpu.CompilerParams(vmem_limit_bytes=limit << 20),
        cost_estimate=pl.CostEstimate(flops=us * 10**9, bytes_accessed=0, transcendentals=0),
        name=kernel.__name__,
    )(*(o for _, o in operands))


def shards(
    features, active, neighbours, first_weight, second_weight, film_scale, film_shift, cotangent
):
    def messages(arrays):
        return [(VMEM, shape((n * arrays, 64, 128))) for n in (4, 4, 1, 1)]


    values, *outgoing = call(
        first_kernel,
        [(HBM, t) for t in (neighbours, features, cotangent, active)],
        [(VMEM, shape((512, 512)))] + messages(2),
        [
            pltpu.VMEM((2, 24, 64, 128), BF),
            pltpu.VMEM((512, 768), BF),
            pltpu.SMEM((4, 26), jnp.int32),
            pltpu.VMEM((4, 64, 512), BF),
            pltpu.VMEM((4, 64, 512), BF),
            pltpu.VMEM((4, 512), jnp.int32),
            pltpu.SMEM((288,), jnp.int32),
            pltpu.SemaphoreType.DMA((4,)),
        ],
        56,
        4,
    )
    arrived = second_round(*first_round(*outgoing[:2]), *outgoing[2:], outgoing[2])
    index, send_ids = call(
        tables_kernel,
        [(HBM, neighbours), (ANY, arrived[0])],
        [(SMEM, shape((104,), jnp.int32)), (SMEM, shape((288,), jnp.int32))],
        [
            pltpu.SMEM((4, 26), jnp.int32),
            pltpu.SMEM((10,), jnp.int32),
            pltpu.SMEM((240,), jnp.int32),
            pltpu.SemaphoreType.DMA,
        ],
        8,
        3,
    )
    spread_shapes = [(512, 1024), (512, 256), (256, 1152)]
    prepared = call(
        prepare_kernel,
        [
            (VMEM, t)
            for t in (
                values,
                active,
                first_weight,
                second_weight,
                film_scale.reshape(1, 64),
                film_shift.reshape(1, 64),
            )
        ],
        [(VMEM, shape((2, 24, 64, 128))), (VMEM, shape((4, 512), F32))]
        + [(VMEM, shape((192, 576)))] * 2
        + [(VMEM, shape((64, 128), F32))] * 2
        + [(VMEM, shape(dims)) for dims in spread_shapes],
        [],
        16,
        3,
    )
    faces, mask, w_first, w_back, gain, shift, *spreads = prepared

    hidden, sums = call(
        second_kernel,
        [(SMEM, index)]
        + [(VMEM, t) for t in (values, faces, *arrived, mask, w_first, w_back, gain, shift)]
        + [(VMEM, t) for t in spreads],
        [
            (VMEM, shape((256, 512))),
            (ANY, shape((2048, 128))),
        ],
        [
            pltpu.VMEM((2, 45, 64, 128), BF),
            pltpu.VMEM((512, 1280), BF),
            pltpu.VMEM((512, 384), BF),
            pltpu.VMEM((512, 512), BF),
            pltpu.VMEM((576, 2560), BF),
            pltpu.VMEM((576, 2560), BF),
            pltpu.VMEM((192, 2560), BF),
            pltpu.VMEM((192, 2560), BF),
            pltpu.VMEM((2048, 128), BF),
            pltpu.SemaphoreType.DMA((3,)),
        ],
        32,
        10,
    )
    parts = lax.all_to_all(sums.reshape(128, 16, 128), AXES, 0, 0, tiled=True)
    hidden_faces, *outgoing = call(
        faces_kernel,
        [(SMEM, send_ids), (VMEM, hidden)],
        [(VMEM, shape((24, 64, 128)))] + messages(1),
        [],
        16,
        8,
    )
    sides = first_round(*outgoing[:2])
    (shares,) = call(
        share_kernel, [(VMEM, parts)] + [(ANY, t) for t in sides], [(VMEM, shape((128, 16, 128)))], [], 16, 1
    )
    arrived = second_round(*sides, *outgoing[2:], shares)
    sums = lax.all_to_all(shares, AXES, 0, 0, tiled=True)
    (block_output,) = call(
        third_kernel,
        [(SMEM, index)]
        + [(VMEM, t) for t in (hidden_faces, *arrived, hidden, active, features, second_weight)],
        [(VMEM, shape((4, 64, 512)))],
        [
            pltpu.VMEM((1, 45, 64, 128), BF),
            pltpu.VMEM((256, 1280), BF),
            pltpu.VMEM((256, 384), BF),
            pltpu.VMEM((256, 512), BF),
            pltpu.VMEM((576, 2560), BF),
            pltpu.VMEM((192, 576), BF),
        ]
        + [pltpu.VMEM(dims, BF) for dims in spread_shapes],
        16,
        2,
    )
    grad_first, grad_second = call(
        unpack_kernel,
        [(VMEM, sums.reshape(2048, 128))],
        [(ANY, shape((27, 64, 64), F32))] * 2,
        [
            pltpu.VMEM((27, 64, 64), F32),
            pltpu.VMEM((27, 64, 64), F32),
            pltpu.SemaphoreType.DMA((6,)),
        ],
        16,
        0,
    )
    return block_output, grad_first, grad_second


def solution(mesh):
    split = P(AXES, None, None)
    rows = P(AXES, None)
    return jax.shard_map(
        shards,
        mesh=mesh,
        in_specs=(split, rows, rows, P(), P(), P(), P(), split),
        out_specs=(split, P(), P()),
        check_vma=False,
    )
```

```python
import jax
import jax.numpy as jnp
from jax import lax
from jax.experimental import pallas as pl
from jax.experimental.pallas import tpu as pltpu
from jax.sharding import PartitionSpec as P

AXES = ("region", "brick")
GRID_X = 8
ZERO_ROW = 44
ARRIVALS = {
    (-1, 0): (24, 4),
    (1, 0): (28, 4),
    (0, -1): (32, 2),
    (-1, -1): (34, 2),
    (1, -1): (36, 2),
    (0, 1): (38, 2),
    (-1, 1): (40, 2),
    (1, 1): (42, 2),
}
BF = jnp.bfloat16
F32 = jnp.float32


def direction_list():
    return [
        (a, b, c)
        for a in (-1, 0, 1)
        for b in (-1, 0, 1)
        for c in (-1, 0, 1)
        if (a, b, c) != (0, 0, 0)
    ]


DIRECTIONS = direction_list()


def face_of(vector):
    if vector[0] != 0:
        return 0 if vector[0] < 0 else 1
    if vector[1] != 0:
        return 2 if vector[1] < 0 else 3
    return 4 if vector[2] < 0 else 5


SEND_FACE = [face_of(d) for d in DIRECTIONS]
READ_FACE = [face_of(tuple(-t for t in d)) for d in DIRECTIONS]


X_TILES = [(0, 0), (0, None), (None, 0), (None, None)]
Y_TILES = [(0, 0), (0, None)]


def one_hot(rows, source):
    at = lax.broadcasted_iota(jnp.int32, (rows, source.shape[1]), 0)
    return jnp.where(at == source, 1.0, 0.0).astype(BF)


def lanes(count):
    return lax.broadcasted_iota(jnp.int32, (1, count), 1)


def face_matrix():
    lane = lanes(768)
    face, u, v = lane >> 7, (lane >> 3) & 7, lane & 7
    first = jnp.where(face < 2, u * 8 + v, jnp.where(face < 4, u * 64 + v, u * 64 + v * 8))
    far = jnp.where(face == 1, 448, jnp.where(face == 3, 56, jnp.where(face == 5, 7, 0)))
    return one_hot(512, first + far)


def padded_lane(count):
    lane = lanes(count)
    cell = lane & 127
    y = (cell * 205) >> 11
    return lane >> 7, y, cell - y * 10


def window_matrix():
    lane = lanes(1152)
    tap, plane, y, z = lane >> 7, (lane >> 6) & 1, (lane >> 3) & 7, lane & 7
    j = jnp.where(tap < 3, 0, jnp.where(tap < 6, 1, 2))
    return one_hot(256, plane * 128 + (y + j) * 10 + z + tap - 3 * j)


def yz_matrix():
    x, y, z = padded_lane(1024)
    y_edge, z_edge = (y == 0) | (y == 9), (z == 0) | (z == 9)
    z_cell = jnp.where(z == 0, 7, jnp.where(z == 9, 0, z - 1))
    from_y = jnp.where(z_edge, 128, 0) + jnp.where(y == 0, 64, 0) + x * 8 + z_cell
    from_z = 256 + jnp.where(z == 0, 64, 0) + x * 8 + y - 1
    own = 384 + (x & 1) * 64 + (y - 1) * 8 + z - 1
    source = jnp.where(y_edge, from_y, jnp.where(z_edge, from_z, own))
    return one_hot(512, jnp.where(y < 10, source, -1))


def x_matrix():
    side, y, z = padded_lane(256)
    y_edge, z_edge = (y == 0) | (y == 9), (z == 0) | (z == 9)
    y_cell = jnp.where(y == 0, 7, jnp.where(y == 9, 0, y - 1))
    z_cell = jnp.where(z == 0, 7, jnp.where(z == 9, 0, z - 1))
    tile = jnp.where(y_edge, 256, 0) + jnp.where(z_edge, 128, 0)
    source = tile + jnp.where(side == 0, 64, 0) + y_cell * 8 + z_cell
    return one_hot(512, jnp.where(y < 10, source, -1))


def dot(a, b):
    return lax.dot_general(a, b, (((1,), (0,)), ((), ())), preferred_element_type=F32)


def dot_nt(a, b):
    return lax.dot_general(a, b, (((1,), (1,)), ((), ())), preferred_element_type=F32)


def low_half(shape):
    return lax.broadcasted_iota(jnp.int32, shape, len(shape) - 1) < 64


def place(n, origin):
    return jnp.where(n >= 0, ((n >> 5) & 3) * 3 + ((n >> 2) & 7) + origin, 9)


def own_origin():
    mine = lax.axis_index("brick")
    return 4 - (mine >> 3) * 3 - (mine & 7)


def choose_sends(neighbours, send_ref, seen=None):
    origin = own_origin()
    readers = []
    for b in range(4):
        bits = [0] * 6
        for e in range(26):
            n = neighbours[b, e]
            where = place(n, origin)
            bits[SEND_FACE[e]] = bits[SEND_FACE[e]] | jnp.left_shift(1, where)
            if seen is not None:
                seen(b, e, n, where)
        readers += bits
    for x, y in ARRIVALS:
        s = (y + 1) * 3 + x + 1
        for t in range(4):
            send_ref[s * 32 + t] = 0
        sent = s * 32
        for f in range(24):
            send_ref[sent] = f
            sent = sent + ((readers[f] >> s) & 1)


def tables_kernel(
    neighbours_any, after_any, index_ref, send_ref, neighbours, held, rank_ref, sem
):
    copy = pltpu.make_async_copy(neighbours_any, neighbours, sem)
    copy.start()
    for s in range(10):
        held[s] = 0
    for f in range(24):
        rank_ref[4 * 24 + f] = f
        rank_ref[9 * 24 + f] = ZERO_ROW
    rows = {}

    def mark(b, e, n, where):
        face = (n & 3) * 6 + READ_FACE[e]
        rows[b, e] = where * 24 + face
        held[where] = held[where] | jnp.left_shift(1, face)

    copy.wait()
    choose_sends(neighbours, send_ref, mark)
    for (x, y), (base, count) in ARRIVALS.items():
        s = (y + 1) * 3 + x + 1
        bits = held[s]
        got = base
        for f in range(24):
            rank_ref[s * 24 + f] = jnp.minimum(got, base + count - 1)
            got = got + ((bits >> f) & 1)
    for (b, e), row in rows.items():
        index_ref[b * 26 + e] = rank_ref[row]


def send_slots(send_ref, x, y):
    s = (y + 1) * 3 + x + 1
    return [send_ref[s * 32 + t] for t in range(4 if y == 0 else 2)]


def pack(send_ref, tiles_of, right_ref, left_ref, up_ref, down_ref):
    for ref, x in ((right_ref, 1), (left_ref, -1)):
        ids = send_slots(send_ref, x, 0) + send_slots(send_ref, x, -1) + send_slots(send_ref, x, 1)
        for t, tile in enumerate(tiles_of(ids)):
            ref[t] = tile
    for ref, y in ((up_ref, 1), (down_ref, -1)):
        for t, tile in enumerate(tiles_of(send_slots(send_ref, 0, y))):
            ref[t] = tile


def own_faces(values, matrix, faces_ref):
    faces = dot(values[...], matrix).astype(BF)
    for a in range(2):
        for b in range(4):
            for f in range(6):
                row = (a * 4 + b) * 64
                faces_ref[a, b * 6 + f] = faces[row : row + 64, f * 128 : f * 128 + 128]


def first_kernel(
    neighbours_any, features_any, cotangent_any, active_any,
    values_ref, right_ref, left_ref, up_ref, down_ref,
    faces_ref, face_mat, neighbours, features, cotangent, active, send_ref, sems,
):
    pairs = (
        (neighbours_any, neighbours), (features_any, features), (cotangent_any, cotangent),
        (active_any, active),
    )
    copies = [pltpu.make_async_copy(s, d, sems.at[t]) for t, (s, d) in enumerate(pairs)]
    for copy in copies:
        copy.start()
    face_mat[...] = face_matrix()
    for copy in copies:
        copy.wait()
    choose_sends(neighbours, send_ref)
    for b in range(4):
        mask = active[b : b + 1, :].astype(F32)
        f = features[b].astype(F32)
        values_ref[b * 64 : b * 64 + 64, :] = (mask * (f / (1.0 + jnp.exp(-f)))).astype(BF)
        values_ref[256 + b * 64 : 320 + b * 64, :] = (mask * cotangent[b].astype(F32)).astype(BF)
    own_faces(values_ref, face_mat[...], faces_ref)
    low = low_half((64, 128))
    pack(
        send_ref,
        lambda ids: [jnp.where(low, faces_ref[0, i], faces_ref[1, i]) for i in ids],
        right_ref, left_ref, up_ref, down_ref,
    )


def as_column(row):
    here = lax.broadcasted_iota(jnp.int32, (64, 64), 0)
    there = lax.broadcasted_iota(jnp.int32, (64, 64), 1)
    picked = jnp.where(here == there, jnp.broadcast_to(row, (64, 64)), 0.0)
    return jnp.broadcast_to(jnp.sum(picked, axis=1, keepdims=True), (64, 128))


def prepare_kernel(
    values, active, first, second, scale, shift,
    faces_ref, mask_ref, w_first, w_back, gain_ref, shift_ref, e_yz, e_x, windows,
):
    own_faces(values, face_matrix(), faces_ref)
    mask_ref[...] = active[...].astype(F32)
    e_yz[...], e_x[...], windows[...] = yz_matrix(), x_matrix(), window_matrix()
    gain_ref[...] = 1.0 + as_column(scale[...])
    shift_ref[...] = as_column(shift[...])
    for i in range(3):
        for jl in range(9):
            k = 9 * i + jl
            rows, lanes = slice(i * 64, i * 64 + 64), slice(jl * 64, jl * 64 + 64)
            w_first[rows, lanes] = first[k]
            w_back[rows, lanes] = second[26 - k].T


def fill_table(table, faces, arrays, groups):
    low = low_half((64, 128))
    for a in range(arrays):
        for f in range(24):
            table[a, f] = faces[a, f] if arrays == 2 else faces[f]
        table[a, ZERO_ROW] = jnp.zeros((64, 128), BF)
    for ref, base, count in groups:
        for t in range(count * arrays // 2):
            tile = ref[t]
            swapped = jnp.concatenate([tile[:, 64:], tile[:, :64]], axis=1)
            first, second = jnp.where(low, tile, swapped), jnp.where(low, swapped, tile)
            if arrays == 2:
                table[0, base + t], table[1, base + t] = first, second
            else:
                table[0, base + 2 * t], table[0, base + 2 * t + 1] = first, second


def build_padded(index_ref, table, values, ext, side_yz, side_x, e_yz, e_x, arrays):
    lane = lax.broadcasted_iota(jnp.int32, (64, 128), 1)
    low, u_far, v_far = lane < 64, (lane & 32) != 0, (lane & 4) != 0
    for a in range(arrays):
        for b in range(4):
            row = (a * 4 + b) * 64

            def face(*offset):
                return table[a, index_ref[b * 26 + DIRECTIONS.index(offset)]]

            def both(low_face, high_face):
                return jnp.where(low, low_face, high_face)

            def along_v(u, v, make):
                if v is None:
                    return jnp.where(v_far, make(u, -1), make(u, 1))
                return make(u, v)

            def tile(u, v, make):
                if u is None:
                    return jnp.where(u_far, along_v(-1, v, make), along_v(1, v, make))
                return along_v(u, v, make)

            def x_faces(y, z):
                return both(face(1, y, z), face(-1, y, z))

            for t, (y, z) in enumerate(X_TILES):
                side_x[row : row + 64, t * 128 : t * 128 + 128] = tile(y, z, x_faces)

            def y_faces(_, z):
                return both(face(0, 1, z), face(0, -1, z))

            for t, (_, z) in enumerate(Y_TILES):
                side_yz[row : row + 64, t * 128 : t * 128 + 128] = along_v(0, z, y_faces)
            side_yz[row : row + 64, 256:384] = both(face(0, 0, 1), face(0, 0, -1))
    outer = dot(side_x[...], e_x[...]).astype(BF)
    ext[:, 0:128] = outer[:, 0:128]
    ext[:, 1152:1280] = outer[:, 128:256]
    for m in range(4):
        known = jnp.concatenate([side_yz[...], values[:, m * 128 : m * 128 + 128]], axis=1)
        inner = dot(known, e_yz[:, m * 256 : m * 256 + 256])
        ext[:, 128 + m * 256 : 384 + m * 256] = inner.astype(BF)


def columns(ext, windows, cols):
    for m in range(5):
        moved = dot(ext[:, m * 256 : m * 256 + 256], windows[...]).astype(BF)
        for a, col in enumerate(cols):
            for b in range(4):
                row = (a * 4 + b) * 64
                lane = b * 640 + m * 128
                for k in range(9):
                    col[k * 64 : k * 64 + 64, lane : lane + 128] = moved[
                        row : row + 64, k * 128 : k * 128 + 128
                    ]


def three_planes(product, lane):
    return (
        product[0:64, lane : lane + 512]
        + product[64:128, lane + 64 : lane + 576]
        + product[128:192, lane + 128 : lane + 640]
    )


def stack_planes(stack, lane, values):
    none = jnp.zeros((64, 64), BF)
    wide = jnp.zeros((64, 128), BF)
    stack[0:64, lane : lane + 640] = jnp.concatenate([values, wide], axis=1)
    stack[64:128, lane : lane + 640] = jnp.concatenate([none, values, none], axis=1)
    stack[128:192, lane : lane + 640] = jnp.concatenate([wide, values], axis=1)


def second_kernel(
    index_ref, values, faces, from_left, from_right, from_up, from_down, mask_ref,
    w_first, w_back, gain_ref, shift_ref, e_yz, e_x, windows,
    hidden_ref, sums_any,
    table, ext, side_yz, side_x, col_a, col_s, stack_h, stack_s, sums_ref, sems,
):
    copies = []

    def send(start, stop, t):
        rows = pl.ds(start, stop - start)
        copies.append(pltpu.make_async_copy(sums_ref.at[rows], sums_any.at[rows], sems.at[t]))
        copies[-1].start()

    sums_ref[1728:2048, :] = jnp.zeros((320, 128), BF)
    send(1728, 2048, 0)
    groups = ((from_left, 24, 4), (from_right, 28, 4), (from_up, 32, 6), (from_down, 38, 6))
    fill_table(table, faces, 2, groups)
    build_padded(index_ref, table, values, ext, side_yz, side_x, e_yz, e_x, 2)
    columns(ext, windows, (col_a, col_s))
    gain = gain_ref[:, 0:1]
    shift = shift_ref[:, 0:1]
    for pair in range(2):
        these = slice(pair * 1280, pair * 1280 + 1280)
        first = dot(w_first[...], col_a[:, these])
        second = dot(w_back[...], col_s[:, these])
        for half in range(2):
            b = 2 * pair + half
            pre, back = three_planes(first, half * 640), three_planes(second, half * 640)
            mask = mask_ref[b : b + 1, :]
            shaped = pre * gain + shift
            gate = 1.0 / (1.0 + jnp.exp(-shaped))
            hidden = (mask * (shaped * gate)).astype(BF)
            slope = (back * mask * gate * (1.0 + shaped * (1.0 - gate)) * gain).astype(BF)
            hidden_ref[b * 64 : b * 64 + 64, :] = hidden
            stack_planes(stack_h, b * 640, hidden)
            stack_planes(stack_s, b * 640, slope)
    pack_sums(dot_nt(col_s[...], stack_h[...]), sums_ref, 0)
    send(0, 864, 1)
    pack_sums(dot_nt(col_a[...], stack_s[...]), sums_ref, 864)
    send(864, 1728, 2)
    for copy in copies:
        copy.wait()


def faces_kernel(
    send_ref, hidden,
    hidden_faces, right_ref, left_ref, up_ref, down_ref,
):
    out = dot(hidden[...], face_matrix()).astype(BF)
    for b in range(4):
        for f in range(6):
            hidden_faces[b * 6 + f] = out[b * 64 : b * 64 + 64, f * 128 : f * 128 + 128]
    low = low_half((64, 128))
    pack(
        send_ref,
        lambda ids: [
            jnp.where(low, hidden_faces[i], hidden_faces[j]) for i, j in zip(ids[::2], ids[1::2])
        ],
        right_ref, left_ref, up_ref, down_ref,
    )


def pack_sums(total, sums_ref, base):
    sums_ref[base : base + 576, :] = total[:, 0:128].astype(BF)
    sums_ref[base + 576 : base + 864, :] = jnp.concatenate(
        [total[0:288, 128:192], total[288:576, 128:192]], axis=1
    ).astype(BF)


def third_kernel(
    index_ref, hidden_faces, from_left, from_right, from_up, from_down, hidden,
    active, features, weight,
    out_ref,
    table, ext, side_yz, side_x, col, w_second, e_yz, e_x, windows,
):
    e_yz[...], e_x[...], windows[...] = yz_matrix(), x_matrix(), window_matrix()
    for i in range(3):
        for jl in range(9):
            w_second[i * 64 : i * 64 + 64, jl * 64 : jl * 64 + 64] = weight[9 * i + jl]
    groups = ((from_left, 24, 4), (from_right, 28, 4), (from_up, 32, 6), (from_down, 38, 6))
    fill_table(table, hidden_faces, 1, groups)
    build_padded(index_ref, table, hidden, ext, side_yz, side_x, e_yz, e_x, 1)
    columns(ext, windows, (col,))
    for pair in range(2):
        product = dot(w_second[...], col[:, pair * 1280 : pair * 1280 + 1280])
        for half in range(2):
            b = 2 * pair + half
            second = active[b : b + 1, :].astype(F32) * three_planes(product, half * 640)
            out_ref[b] = (features[b].astype(F32) + second).astype(BF)


def share_kernel(parts, left_any, right_any, out_ref):
    totals = [parts[d].astype(F32) for d in range(4)]
    for d in range(4, 128):
        totals[d % 4] = totals[d % 4] + parts[d].astype(F32)
    total = ((totals[0] + totals[1]) + (totals[2] + totals[3])).astype(BF)
    for d in range(128):
        out_ref[d] = total


def unpack_kernel(sums, first_any, second_any, first, second, sems):
    copies = []
    for t, (grad, grad_any) in enumerate(((second, second_any), (first, first_any))):
        base = t * 864
        for i in range(3):
            for jl in range(9):
                if i < 2:
                    block = sums[base + jl * 64 : base + jl * 64 + 64, i * 64 : i * 64 + 64]
                else:
                    pieces = []
                    for r in (jl * 64, jl * 64 + 32):
                        lane, at = (0, r) if r < 288 else (64, r - 288)
                        at += base + 576
                        pieces.append(sums[at : at + 32, lane : lane + 64])
                    block = jnp.concatenate(pieces, axis=0)
                block = block.astype(F32)
                k = 9 * i + jl
                if t == 0:
                    grad[26 - k] = block
                else:
                    grad[k] = block.T
                if jl % 3 == 2:
                    three = pl.ds(26 - k if t == 0 else k - 2, 3)
                    copies.append(
                        pltpu.make_async_copy(
                            grad.at[three], grad_any.at[three], sems.at[len(copies)]
                        )
                    )
                    copies[-1].start()
    for copy in copies:
        copy.wait()


def sent(array, step):
    pairs = []
    for i in range(32):
        j = i + step
        if 0 <= j < 32 and (abs(step) == GRID_X or i // GRID_X == j // GRID_X):
            pairs.append((i, j))
    return lax.ppermute(array, "brick", pairs)


def forward_kernel(from_left, from_right, up, down, after_any, up_ref, down_ref):
    n = up.shape[0]
    up_ref[0:n] = up[...]
    down_ref[0:n] = down[...]
    for t, ref in enumerate((from_left, from_right)):
        up_ref[n + t * n : 2 * n + t * n] = ref[3 * n :]
        down_ref[n + t * n : 2 * n + t * n] = ref[2 * n : 3 * n]


def first_round(right, left):
    return sent(right, 1), sent(left, -1)


def second_round(from_left, from_right, up, down, after):
    upward, downward = call(
        forward_kernel,
        [(VMEM, t) for t in (from_left, from_right, up, down)] + [(ANY, after)],
        [(VMEM, shape((3 * up.shape[0], 64, 128)))] * 2,
        [],
        8,
        0,
    )
    return from_left, from_right, sent(upward, GRID_X), sent(downward, -GRID_X)


def shape(dims, dtype=BF):
    return jax.ShapeDtypeStruct(dims, dtype)


SMEM = pl.BlockSpec(memory_space=pltpu.SMEM)
VMEM = pl.BlockSpec(memory_space=pltpu.VMEM)
ANY = pl.BlockSpec(memory_space=pl.ANY)
HBM = pl.BlockSpec(memory_space=pltpu.HBM)


def call(kernel, operands, outs, scratch, limit, us):
    return pl.pallas_call(
        kernel,
        out_shape=tuple(o for _, o in outs),
        in_specs=[s for s, _ in operands],
        out_specs=tuple(s for s, _ in outs),
        scratch_shapes=scratch,
        compiler_params=pltpu.CompilerParams(vmem_limit_bytes=limit << 20),
        cost_estimate=pl.CostEstimate(flops=us * 10**9, bytes_accessed=0, transcendentals=0),
        name=kernel.__name__,
    )(*(o for _, o in operands))


def shards(
    features, active, neighbours, first_weight, second_weight, film_scale, film_shift, cotangent
):
    def messages(arrays):
        return [(VMEM, shape((n * arrays, 64, 128))) for n in (4, 4, 1, 1)]


    values, *outgoing = call(
        first_kernel,
        [(HBM, t) for t in (neighbours, features, cotangent, active)],
        [(VMEM, shape((512, 512)))] + messages(2),
        [
            pltpu.VMEM((2, 24, 64, 128), BF),
            pltpu.VMEM((512, 768), BF),
            pltpu.SMEM((4, 26), jnp.int32),
            pltpu.VMEM((4, 64, 512), BF),
            pltpu.VMEM((4, 64, 512), BF),
            pltpu.VMEM((4, 512), jnp.int32),
            pltpu.SMEM((288,), jnp.int32),
            pltpu.SemaphoreType.DMA((4,)),
        ],
        56,
        4,
    )
    arrived = second_round(*first_round(*outgoing[:2]), *outgoing[2:], outgoing[2])
    index, send_ids = call(
        tables_kernel,
        [(HBM, neighbours), (ANY, arrived[0])],
        [(SMEM, shape((104,), jnp.int32)), (SMEM, shape((288,), jnp.int32))],
        [
            pltpu.SMEM((4, 26), jnp.int32),
            pltpu.SMEM((10,), jnp.int32),
            pltpu.SMEM((240,), jnp.int32),
            pltpu.SemaphoreType.DMA,
        ],
        8,
        3,
    )
    spread_shapes = [(512, 1024), (512, 256), (256, 1152)]
    prepared = call(
        prepare_kernel,
        [
            (VMEM, t)
            for t in (
                values,
                active,
                first_weight,
                second_weight,
                film_scale.reshape(1, 64),
                film_shift.reshape(1, 64),
            )
        ],
        [(VMEM, shape((2, 24, 64, 128))), (VMEM, shape((4, 512), F32))]
        + [(VMEM, shape((192, 576)))] * 2
        + [(VMEM, shape((64, 128), F32))] * 2
        + [(VMEM, shape(dims)) for dims in spread_shapes],
        [],
        16,
        3,
    )
    faces, mask, w_first, w_back, gain, shift, *spreads = prepared

    hidden, sums = call(
        second_kernel,
        [(SMEM, index)]
        + [(VMEM, t) for t in (values, faces, *arrived, mask, w_first, w_back, gain, shift)]
        + [(VMEM, t) for t in spreads],
        [
            (VMEM, shape((256, 512))),
            (ANY, shape((2048, 128))),
        ],
        [
            pltpu.VMEM((2, 45, 64, 128), BF),
            pltpu.VMEM((512, 1280), BF),
            pltpu.VMEM((512, 384), BF),
            pltpu.VMEM((512, 512), BF),
            pltpu.VMEM((576, 2560), BF),
            pltpu.VMEM((576, 2560), BF),
            pltpu.VMEM((192, 2560), BF),
            pltpu.VMEM((192, 2560), BF),
            pltpu.VMEM((2048, 128), BF),
            pltpu.SemaphoreType.DMA((3,)),
        ],
        32,
        10,
    )
    parts = lax.all_to_all(sums.reshape(128, 16, 128), AXES, 0, 0, tiled=True)
    hidden_faces, *outgoing = call(
        faces_kernel,
        [(SMEM, send_ids), (VMEM, hidden)],
        [(VMEM, shape((24, 64, 128)))] + messages(1),
        [],
        16,
        8,
    )
    sides = first_round(*outgoing[:2])
    (shares,) = call(
        share_kernel, [(VMEM, parts)] + [(ANY, t) for t in sides], [(VMEM, shape((128, 16, 128)))], [], 16, 1
    )
    arrived = second_round(*sides, *outgoing[2:], shares)
    sums = lax.all_to_all(shares, AXES, 0, 0, tiled=True)
    (block_output,) = call(
        third_kernel,
        [(SMEM, index)]
        + [(VMEM, t) for t in (hidden_faces, *arrived, hidden, active, features, second_weight)],
        [(VMEM, shape((4, 64, 512)))],
        [
            pltpu.VMEM((1, 45, 64, 128), BF),
            pltpu.VMEM((256, 1280), BF),
            pltpu.VMEM((256, 384), BF),
            pltpu.VMEM((256, 512), BF),
            pltpu.VMEM((576, 2560), BF),
            pltpu.VMEM((192, 576), BF),
        ]
        + [pltpu.VMEM(dims, BF) for dims in spread_shapes],
        16,
        2,
    )
    grad_first, grad_second = call(
        unpack_kernel,
        [(VMEM, sums.reshape(2048, 128))],
        [(ANY, shape((27, 64, 64), F32))] * 2,
        [
            pltpu.VMEM((27, 64, 64), F32),
            pltpu.VMEM((27, 64, 64), F32),
            pltpu.SemaphoreType.DMA((18,)),
        ],
        16,
        0,
    )
    return block_output, grad_first, grad_second


def solution(mesh):
    split = P(AXES, None, None)
    rows = P(AXES, None)
    return jax.shard_map(
        shards,
        mesh=mesh,
        in_specs=(split, rows, rows, P(), P(), P(), P(), split),
        out_specs=(split, P(), P()),
        check_vma=False,
    )
```
